256 devices in a mesh: rows: 32 (over z_lo, y, core), rep: 8 (over x, z_hi).
Axes of the slice: x: 4, y: 4, z: 8 (z_hi: 2, z_lo: 4; z = z_hi * 4 + z_lo), core: 2. Of those that a mesh axis runs over, the one named last changes fastest.
Arguments:
- features: bfloat16 [16384, 256], P('rows'), may hold values from -6 to 6
- weight: bfloat16 [256, 256], replicated, may hold values from -0.375 to 0.375
- cotangent: bfloat16 [16384, 256], P(('rows', 'rep')), may hold values from -6 to 6
- tile_values: bfloat16 [32, 32, 2, 128, 128], P('rows', 'rep'), may hold values from -1 to 1
- tile_slots: int32 [32, 32, 2], P('rows', 'rep'), may hold values from 0 to 15, as said below
- tile_count: int32 [32, 32], P('rows', 'rep'), may hold values from 1 to 2, as said below
Outputs:
- output: bfloat16 [16384, 256], P(('rows', 'rep'))
- grad_weight: float32 [256, 256], replicated
- grad_features: bfloat16 [16384, 256], P('rows')
The draws below stay inside these ranges and needn't reach their ends.
Inputs may be any that keep to these rules, and one draw needn't show every extreme that they name: `tile_slots`: for each block pair, 2 distinct positions (tile row times 4 plus tile column); only the first tile_count of them are live. `tile_count`: 2 in at least one block pair.
All inputs are finite; a program needn't handle non-finite values.
Results may differ from the reference program's by a relative error of at most 0.0059.
Values may be sent and summed in bfloat16 or wider, within the bound.
No kernel may reach another device: no remote copies, remote signals or barrier semaphores. Data moves between devices by JAX's collectives and lax.ppermute only.
A program may use at most 64 MiB of HBM per device.

```python
import jax
import jax.numpy as jnp
from jax import lax

WIDTH = 256
TILE = 128
BLOCK_NODES = 512
TILE_ROWS = 4
TILES_MAX = 2
NODES = 16384
N_ROWS = 32


def draw_tile_slots(key, part):
    key = jax.random.fold_in(key, 11)
    chosen = jax.random.randint(jax.random.fold_in(key, 1), (), 0, N_ROWS * N_ROWS)
    pair_keys = jax.random.split(jax.random.fold_in(key, 2), N_ROWS * N_ROWS)
    positions = TILE_ROWS * TILE_ROWS

    def one_pair(pair_key, pair_index):
        ordering = jax.random.permutation(pair_key, positions)[:TILES_MAX]
        offset_value = jnp.where(pair_index == chosen, positions - 1 - ordering[0], 0)
        return (ordering + offset_value) % positions
    slot_table = jax.vmap(one_pair)(pair_keys, jnp.arange(N_ROWS * N_ROWS))
    return slot_table.reshape(N_ROWS, N_ROWS, TILES_MAX).astype(jnp.int32)


def draw_tile_count(key, part):
    key = jax.random.fold_in(key, 23)
    counts_flat = jax.random.randint(jax.random.fold_in(key, 1), (N_ROWS * N_ROWS,), 1, TILES_MAX + 1)
    chosen = jax.random.randint(jax.random.fold_in(key, 2), (), 0, N_ROWS * N_ROWS)
    counts_flat = jnp.where(jnp.arange(N_ROWS * N_ROWS) == chosen, TILES_MAX, counts_flat)
    return counts_flat.reshape(N_ROWS, N_ROWS).astype(jnp.int32)


def draw_tile_values(key, part):
    key = jax.random.fold_in(key, 37)
    full_shape = (N_ROWS, N_ROWS, TILES_MAX, TILE, TILE)
    per_row = N_ROWS * (TILES_MAX + 1) / (2.0 * TILE_ROWS) * (4.0 + TILE / 8.0)
    scale = 1.0 / (3.0 * per_row ** 0.5)
    scale = min(scale, 1.0 / 6.0)
    edge_mask = jax.random.randint(jax.random.fold_in(key, 1), full_shape, 0, 8) == 0
    shifts = jax.random.randint(jax.random.fold_in(key, 2), (N_ROWS, N_ROWS, TILES_MAX, 1, 1), 0, TILE)
    row_ids = jnp.arange(TILE)[:, None]
    col_ids = jnp.arange(TILE)[None, :]
    on_diagonal = (row_ids + shifts) % TILE == col_ids
    raw = jnp.clip(jax.random.normal(jax.random.fold_in(key, 3), full_shape, jnp.float32), -3.0, 3.0)
    signs = jnp.where(raw >= 0.0, 1.0, -1.0)
    diagonal_part = signs * (1.0 + jnp.abs(raw)) * 1.5
    values = jnp.where(on_diagonal, diagonal_part, jnp.where(edge_mask, raw, 0.0)) * scale
    return values.astype(jnp.float32).astype(jnp.bfloat16)


def block_levels(stream_key, shape, cuts, low, high):
    def one(position, parts):
        heights = jax.random.uniform(jax.random.fold_in(jax.random.fold_in(stream_key, 6), position), (parts,), jnp.float32, low / len(cuts), high / len(cuts))
        return jnp.repeat(jnp.exp(heights), shape[position] // parts).reshape((-1,) + (1,) * (len(shape) - position - 1))

    level = one(*cuts[0])
    for cut in cuts[1:]:
        level = level * one(*cut)
    return level


def centred(key, shape, spread, limit, pieces=(), dtype=jnp.bfloat16):
    entries = spread * jax.random.normal(key, shape, jnp.float32)
    if pieces:
        entries = entries * block_levels(key, shape, pieces, -0.22, 0.18)
    return jnp.clip(entries, -limit, limit).astype(dtype)


def setup_inputs(seed: int = 0) -> dict:
    streams_of = jax.random.split(jax.random.key(seed), 7)
    features = centred(streams_of[0], (NODES, WIDTH), 1.0, 6.0, ((0, 32),))
    weight = centred(streams_of[1], (WIDTH, WIDTH), WIDTH ** -0.5, 0.375)
    cotangent = centred(streams_of[2], (NODES, WIDTH), 1.0, 6.0, ((0, 256),))
    tile_values = draw_tile_values(jax.random.fold_in(streams_of[6], 71), 0)
    tile_slots = draw_tile_slots(jax.random.fold_in(streams_of[6], 71), 0)
    tile_count = draw_tile_count(jax.random.fold_in(streams_of[6], 71), 0)
    return dict(features=features, weight=weight, cotangent=cotangent, tile_values=tile_values, tile_slots=tile_slots, tile_count=tile_count)


def forward_block(block_index, feature_tiles, tile_values, tile_slots, tile_count):
    values = lax.dynamic_index_in_dim(tile_values, block_index, 0, keepdims=False).astype(jnp.float32)
    slot_ids = lax.dynamic_index_in_dim(tile_slots, block_index, 0, keepdims=False)
    live_tiles = lax.dynamic_index_in_dim(tile_count, block_index, 0, keepdims=False)
    tile_rows = slot_ids // TILE_ROWS
    tile_cols = slot_ids % TILE_ROWS
    panels = feature_tiles[jnp.arange(N_ROWS)[:, None], tile_cols]
    products = jnp.einsum("jkab,jkbf->jkaf", values, panels, precision=lax.Precision.HIGHEST)
    keep_mask = (jnp.arange(TILES_MAX)[None, :] < live_tiles[:, None]).astype(jnp.float32)
    onehot = (tile_rows[:, :, None] == jnp.arange(TILE_ROWS)[None, None, :]).astype(jnp.float32) * keep_mask[:, :, None]
    summed = jnp.einsum("jkn,jkaf->naf", onehot, products, precision=lax.Precision.HIGHEST)
    return summed.reshape(BLOCK_NODES, WIDTH)


def backward_block(block_index, grad_tiles, tile_values, tile_slots, tile_count):
    values = lax.dynamic_index_in_dim(tile_values, block_index, 1, keepdims=False).astype(jnp.float32)
    slot_ids = lax.dynamic_index_in_dim(tile_slots, block_index, 1, keepdims=False)
    live_tiles = lax.dynamic_index_in_dim(tile_count, block_index, 1, keepdims=False)
    tile_rows = slot_ids // TILE_ROWS
    tile_cols = slot_ids % TILE_ROWS
    panels = grad_tiles[jnp.arange(N_ROWS)[:, None], tile_rows]
    products = jnp.einsum("ikab,ikaf->ikbf", values, panels, precision=lax.Precision.HIGHEST)
    keep_mask = (jnp.arange(TILES_MAX)[None, :] < live_tiles[:, None]).astype(jnp.float32)
    onehot = (tile_cols[:, :, None] == jnp.arange(TILE_ROWS)[None, None, :]).astype(jnp.float32) * keep_mask[:, :, None]
    summed = jnp.einsum("ikn,ikbf->nbf", onehot, products, precision=lax.Precision.HIGHEST)
    return summed.reshape(BLOCK_NODES, WIDTH)


def reference(features, weight, cotangent, tile_values, tile_slots, tile_count):
    feature_tiles = features.astype(jnp.float32).reshape(N_ROWS, TILE_ROWS, TILE, WIDTH)
    aggregate = lax.map(lambda block_index: forward_block(block_index, feature_tiles, tile_values, tile_slots, tile_count), jnp.arange(N_ROWS))
    aggregate = aggregate.reshape(NODES, WIDTH).astype(jnp.bfloat16)
    preact = jnp.dot(aggregate, weight, preferred_element_type=jnp.float32)
    gates = jax.nn.sigmoid(preact)
    output = (preact * gates).astype(jnp.bfloat16)
    grad_pre = (cotangent.astype(jnp.float32) * gates * (1.0 + preact * (1.0 - gates))).astype(jnp.bfloat16)
    grad_weight = jnp.dot(aggregate.T, grad_pre, preferred_element_type=jnp.float32)
    grad_agg = jnp.dot(grad_pre, weight.T, preferred_element_type=jnp.float32).astype(jnp.bfloat16)
    grad_tiles = grad_agg.astype(jnp.float32).reshape(N_ROWS, TILE_ROWS, TILE, WIDTH)
    grad_features = lax.map(lambda block_index: backward_block(block_index, grad_tiles, tile_values, tile_slots, tile_count), jnp.arange(N_ROWS))
    grad_features = grad_features.reshape(NODES, WIDTH).astype(jnp.bfloat16)
    return output, grad_weight, grad_features
```

```python
import itertools

import jax
import jax.numpy as jnp
from jax import lax
from jax.experimental import pallas as pl
from jax.experimental.pallas import tpu as pltpu
from jax.sharding import PartitionSpec as P

BF = jnp.bfloat16
F32 = jnp.float32
TILE = 128
WIDTH = 256
BLOCK = 512
PART = 128
SLICE = 64
AXES = ("rows", "rep")


def u_of(y):
    return (y ^ (y >> 1)) & 1


def v_of(y):
    return y >> 1


Y_OF = {(u_of(y), v_of(y)): y for y in range(4)}
PLACES = list(itertools.product(range(4), range(4), range(2), range(4), range(2)))


def index_of(z, y, c, x, h):
    return (z * 8 + y * 2 + c) * 8 + x * 2 + h


def pairs(target):
    return [(index_of(*place), index_of(*target(*place))) for place in PLACES]


FLIP_C = pairs(lambda z, y, c, x, h: (z, y, 1 - c, x, h))
FLIP_U = pairs(lambda z, y, c, x, h: (z, Y_OF[1 - u_of(y), v_of(y)], c, x, h))
FLIP_V = pairs(lambda z, y, c, x, h: (z, Y_OF[u_of(y), 1 - v_of(y)], c, x, h))
FLIP_H = pairs(lambda z, y, c, x, h: (z, y, c, x, 1 - h))
FLIP_X = [pairs(lambda z, y, c, x, h, k=k: (z, y, c, x ^ k, h)) for k in (1, 2, 3)]
FLIP_Z = [pairs(lambda z, y, c, x, h, k=k: (z ^ k, y, c, x, h)) for k in (1, 2, 3)]
TO_COLUMN = pairs(lambda z, y, c, x, h: (x, Y_OF[y & 1, h], c, z, y >> 1))
TO_ROW = [(there, here) for here, there in TO_COLUMN]


def send(value, route):
    return lax.ppermute(value, AXES, route)


def place():
    r = lax.axis_index("rows")
    p = lax.axis_index("rep")
    y = (r >> 1) & 3
    v = y >> 1
    return dict(z=r >> 3, c=r & 1, u=(y ^ v) & 1, v=v, x=p >> 1, h=p & 1)


def at(index, size):
    return pl.ds(pl.multiple_of(index * size, size), size)


def dot(a, b, dims=((1,), (0,))):
    return lax.dot_general(a, b, (dims, ((), ())), preferred_element_type=F32)


def call(body, outs, *args, scalars=0, scratch=()):
    spaces = [pltpu.SMEM] * scalars + [pltpu.VMEM] * (len(args) - scalars)
    return pl.pallas_call(
        body,
        out_shape=[jax.ShapeDtypeStruct(shape, dtype) for shape, dtype in outs],
        in_specs=[pl.BlockSpec(memory_space=space) for space in spaces],
        out_specs=[pl.BlockSpec(memory_space=pltpu.VMEM)] * len(outs),
        scratch_shapes=list(scratch),
        compiler_params=pltpu.CompilerParams(vmem_limit_bytes=16 * 2**20),
    )(*args)


def split(value):
    high = value.astype(BF)
    return high, (value - high.astype(F32)).astype(BF)


def put_split(ref, start, value):
    high, low = split(value)
    ref[start : start + SLICE, :] = high
    ref[start + SLICE : start + 2 * SLICE, :] = low


def get_split(ref, start):
    return ref[start : start + SLICE, :].astype(F32) + ref[start + SLICE : start + 2 * SLICE, :].astype(F32)


def live_tile(slots, count, tiles, b, s):
    slot = slots[b * 2 + s]
    tile = jnp.where(s < count[b], tiles[b * 2 + s], jnp.zeros((), BF))
    return tile, slot >> 2, slot & 3


def forward_body(slots, count, tiles, f0, f1, f2, f3, to1, to2, to3, own, total):
    me = place()
    total[...] = jnp.zeros_like(total)
    for k, block in enumerate((f0, f1, f2, f3)):
        b = (me["u"] * 2 + me["c"]) ^ k
        for s in range(2):
            tile, tile_row, tile_col = live_tile(slots, count, tiles, b, s)
            total[at(tile_row, TILE), :] += dot(tile, block[at(tile_col, TILE), :])
    own[...] = total[at(me["x"], PART), :]
    for k, to in ((1, to1), (2, to2), (3, to3)):
        to[...] = total[at(me["x"] ^ k, PART), :].astype(BF)


def sum_body(own, r1, r2, r3, out):
    out[...] = own[...] + r1[...].astype(F32) + (r2[...].astype(F32) + r3[...].astype(F32))


def layer_body(mine, other, weight, cot, cot_other, output, message):
    me = place()
    aggregate = (mine[...] + other[...]).astype(BF)
    preact = dot(aggregate, weight[...])
    gates = jax.nn.sigmoid(preact)
    activation = (preact * gates).astype(BF)
    first = me["h"] == 0
    output[...] = jnp.where(first, activation[:SLICE], activation[SLICE:])
    a, b = cot[...], cot_other[...]
    cotangent = jnp.concatenate([jnp.where(first, a, b), jnp.where(first, b, a)], axis=0).astype(F32)
    message[0:PART, :] = aggregate
    message[PART:, :] = (cotangent * gates * (1.0 + preact * (1.0 - gates))).astype(BF)


def backward_body(slots, count, tiles, weight, m0, m1, m2, m3, to_c, keep, keep_w, aggregate, grad_pre, grad_agg, grad_w):
    me = place()
    for k, m in enumerate((m0, m1, m2, m3)):
        rows = at(me["x"] ^ k, PART)
        aggregate[rows, :] = m[0:PART, :]
        grad_pre[rows, :] = m[PART:, :]
    grad_agg[...] = dot(grad_pre[...], weight[...], ((1,), (1,))).astype(BF)
    grad_w[...] = dot(aggregate[...], grad_pre[...], ((0,), (0,)))
    share = grad_w[at(me["x"], SLICE), :]
    keep_w[...] = share
    to_c[2 * BLOCK :, :] = share
    for k, (ref, start) in enumerate(((keep, 0), (to_c, 0), (keep, BLOCK), (to_c, BLOCK))):
        b = (me["u"] * 2 + me["c"]) ^ k
        ref[start : start + BLOCK, :] = jnp.zeros((BLOCK, WIDTH), F32)
        for s in range(2):
            tile, tile_row, tile_col = live_tile(slots, count, tiles, b, s)
            rows = pl.ds(pl.multiple_of(start + tile_col * TILE, TILE), TILE)
            ref[rows, :] += dot(tile, grad_agg[at(tile_row, TILE), :], ((0,), (0,)))


def after_c_body(keep, keep_w, got, to_u, own, own_w):
    own[...] = keep[0:BLOCK, :] + got[0:BLOCK, :]
    to_u[0:BLOCK, :] = (keep[BLOCK:, :] + got[BLOCK : 2 * BLOCK, :]).astype(BF)
    share = keep_w[...] + got[2 * BLOCK :, :]
    put_split(to_u, BLOCK, share)
    own_w[...] = share


def after_u_body(own, own_w, got, to1, to2, to3, kept, kept_w, total):
    me = place()
    total[...] = own[...] + got[0:BLOCK, :].astype(F32)
    high, low = split(own_w[...])
    share = (high.astype(F32) + low.astype(F32)) + get_split(got, BLOCK)
    kept[...] = total[at(me["z"], PART), :]
    kept_w[...] = share
    for k, to in ((1, to1), (2, to2), (3, to3)):
        to[0:PART, :] = total[at(me["z"] ^ k, PART), :].astype(BF)
        put_split(to, PART, share)


def after_z_body(kept, kept_w, r1, r2, r3, to_v):
    total = kept[...] + r1[0:PART, :].astype(F32)
    to_v[0:PART, :] = total + (r2[0:PART, :].astype(F32) + r3[0:PART, :].astype(F32))
    high, low = split(kept_w[...])
    share = (high.astype(F32) + low.astype(F32)) + get_split(r1, PART)
    to_v[PART:, :] = share + (get_split(r2, PART) + get_split(r3, PART))


def after_v_body(mine, got, piece, share):
    piece[...] = (mine[0:PART, :] + got[0:PART, :]).astype(BF)
    put_split(share, 0, mine[PART:, :] + got[PART:, :])


def finish_body(p0, p1, p2, p3, w0, w1, w2, w3, grad_features, grad_weight):
    me = place()
    for k, (piece, share) in enumerate(((p0, w0), (p1, w1), (p2, w2), (p3, w3))):
        grad_features[at(me["x"] ^ k, PART), :] = piece[...]
        grad_weight[at(me["x"] ^ k, SLICE), :] = get_split(share, 0)


def on_device(features, weight, cotangent, tile_values, tile_slots, tile_count):
    tiles = tile_values.reshape(8, TILE, TILE)
    slots = tile_slots.reshape(8)
    count = tile_count.reshape(4)

    f0 = send(features, TO_COLUMN)
    cot_other = send(cotangent, FLIP_H)
    f2 = send(f0, FLIP_U)
    f1 = send(f0, FLIP_C)
    f3 = send(f2, FLIP_C)
    part = ((PART, WIDTH), BF)
    part32 = ((PART, WIDTH), F32)
    share32 = ((SLICE, WIDTH), F32)
    *to, own = call(
        forward_body, [part, part, part, part32], slots, count, tiles, f0, f1, f2, f3,
        scalars=2, scratch=[pltpu.VMEM((BLOCK, WIDTH), F32)],
    )
    got = [send(value, route) for value, route in zip(to, FLIP_X)]
    (mine,) = call(sum_body, [part32], own, *got)
    other = send(mine, FLIP_H)
    output, message = call(
        layer_body, [((SLICE, WIDTH), BF), ((2 * PART, WIDTH), BF)], mine, other, weight, cotangent, cot_other
    )
    got = [send(message, route) for route in FLIP_X]
    to_c, keep, keep_w = call(
        backward_body,
        [((2 * BLOCK + SLICE, WIDTH), F32), ((2 * BLOCK, WIDTH), F32), share32],
        slots, count, tiles, weight, message, *got,
        scalars=2,
        scratch=[
            pltpu.VMEM((BLOCK, WIDTH), BF),
            pltpu.VMEM((BLOCK, WIDTH), BF),
            pltpu.VMEM((BLOCK, WIDTH), BF),
            pltpu.VMEM((WIDTH, WIDTH), F32),
        ],
    )
    got = send(to_c, FLIP_C)
    to_u, own, own_w = call(
        after_c_body, [((BLOCK + 2 * SLICE, WIDTH), BF), ((BLOCK, WIDTH), F32), share32], keep, keep_w, got
    )
    got = send(to_u, FLIP_U)
    to_z = ((PART + 2 * SLICE, WIDTH), BF)
    *to, kept, kept_w = call(
        after_u_body, [to_z, to_z, to_z, part32, share32], own, own_w, got,
        scratch=[pltpu.VMEM((BLOCK, WIDTH), F32)],
    )
    got = [send(value, route) for value, route in zip(to, FLIP_Z)]
    (to_v,) = call(after_z_body, [((PART + SLICE, WIDTH), F32)], kept, kept_w, *got)
    got = send(to_v, FLIP_V)
    piece, share = call(after_v_body, [part, ((2 * SLICE, WIDTH), BF)], to_v, got)
    piece = send(piece, TO_ROW)
    shares = [share] + [send(share, route) for route in FLIP_X]
    pieces = [piece] + [send(piece, route) for route in FLIP_X]
    grad_features, grad_weight = call(
        finish_body, [((BLOCK, WIDTH), BF), ((WIDTH, WIDTH), F32)], *pieces, *shares
    )
    return output, grad_weight, grad_features


def solution(mesh):
    placed = (
        P("rows", None),
        P(),
        P(("rows", "rep"), None),
        P("rows", "rep", None, None, None),
        P("rows", "rep", None),
        P("rows", "rep"),
    )
    return jax.shard_map(
        on_device,
        mesh=mesh,
        in_specs=placed,
        out_specs=(P(("rows", "rep"), None), P(), P("rows", None)),
        check_vma=False,
    )
```

```python
import itertools

import jax
import jax.numpy as jnp
from jax import lax
from jax.experimental import pallas as pl
from jax.experimental.pallas import tpu as pltpu
from jax.sharding import PartitionSpec as P

BF = jnp.bfloat16
F32 = jnp.float32
TILE = 128
WIDTH = 256
BLOCK = 512
PART = 128
SLICE = 64
AXES = ("rows", "rep")


def u_of(y):
    return (y ^ (y >> 1)) & 1


def v_of(y):
    return y >> 1


Y_OF = {(u_of(y), v_of(y)): y for y in range(4)}
PLACES = list(itertools.product(range(4), range(4), range(2), range(4), range(2)))


def index_of(z, y, c, x, h):
    return (z * 8 + y * 2 + c) * 8 + x * 2 + h


def pairs(target):
    return [(index_of(*place), index_of(*target(*place))) for place in PLACES]


FLIP_C = pairs(lambda z, y, c, x, h: (z, y, 1 - c, x, h))
FLIP_U = pairs(lambda z, y, c, x, h: (z, Y_OF[1 - u_of(y), v_of(y)], c, x, h))
FLIP_V = pairs(lambda z, y, c, x, h: (z, Y_OF[u_of(y), 1 - v_of(y)], c, x, h))
FLIP_H = pairs(lambda z, y, c, x, h: (z, y, c, x, 1 - h))
FLIP_X = [pairs(lambda z, y, c, x, h, k=k: (z, y, c, x ^ k, h)) for k in (1, 2, 3)]
FLIP_Z = [pairs(lambda z, y, c, x, h, k=k: (z ^ k, y, c, x, h)) for k in (1, 2, 3)]
ROUTE = (((2, 1, 3, 0), (0, 3, 2, 1), (2, 1, 0, 3), (3, 0, 2, 1)), ((0, 1, 3, 2), (0, 1, 2, 3), (0, 1, 2, 3), (1, 0, 2, 3)))
TO_ROW = pairs(lambda z, y, c, x, h: (x, Y_OF[u_of(y), h], c, ROUTE[v_of(y) == h][x][z], 1 - v_of(y)))
TO_COLUMN = [(there, here) for here, there in TO_ROW]


def chunk_table(same):
    word = sum((z << (8 * x + 2 * ROUTE[same][x][z])) for x in range(4) for z in range(4))
    return word - (1 << 32) if word >> 31 else word


CHUNKS = (chunk_table(0), chunk_table(1))


def send(value, route):
    return lax.ppermute(value, AXES, route)


def place():
    r = lax.axis_index("rows")
    p = lax.axis_index("rep")
    y = (r >> 1) & 3
    v = y >> 1
    return dict(z=r >> 3, c=r & 1, u=(y ^ v) & 1, v=v, x=p >> 1, h=p & 1)


def chunk_of(me, x):
    word = jnp.where((1 - me["h"]) == me["v"], jnp.int32(CHUNKS[1]), jnp.int32(CHUNKS[0]))
    return (word >> (8 * me["z"] + 2 * x)) & 3


def at(index, size):
    return pl.ds(pl.multiple_of(index * size, size), size)


def dot(a, b, dims=((1,), (0,))):
    return lax.dot_general(a, b, (dims, ((), ())), preferred_element_type=F32)


SMEM = pl.BlockSpec(memory_space=pltpu.SMEM)
VMEM = pl.BlockSpec(memory_space=pltpu.VMEM)
HBM = pl.BlockSpec(memory_space=pl.ANY)


def call(body, outs, *args, specs=None, scratch=()):
    return pl.pallas_call(
        body,
        out_shape=[jax.ShapeDtypeStruct(shape, dtype) for shape, dtype in outs],
        in_specs=specs or [VMEM] * len(args),
        out_specs=[VMEM] * len(outs),
        scratch_shapes=list(scratch),
        compiler_params=pltpu.CompilerParams(vmem_limit_bytes=24 * 2**20),
    )(*args)


def split(value):
    high = value.astype(BF)
    return high, (value - high.astype(F32)).astype(BF)


def put_split(ref, start, value):
    high, low = split(value)
    ref[start : start + SLICE, :] = high
    ref[start + SLICE : start + 2 * SLICE, :] = low


def get_split(ref, start):
    return ref[start : start + SLICE, :].astype(F32) + ref[start + SLICE : start + 2 * SLICE, :].astype(F32)


def chunk_body(features, out, sem):
    me = place()
    copy = pltpu.make_async_copy(features.at[at(chunk_of(me, me["x"]), PART), :], out, sem)
    copy.start()
    copy.wait()


def dense_body(slots, count, tiles, dense, dense_t):
    me = place()
    dense[...] = jnp.zeros_like(dense)
    dense_t[...] = jnp.zeros_like(dense_t)
    for k in range(4):
        b = ((me["u"] ^ me["h"]) * 2 + me["c"]) ^ k
        for s in range(2):
            slot = slots[0, b, s]
            tile = jnp.where(s < count[0, b], tiles[0, b, s], jnp.zeros((), BF))

            @pl.when(s < count[0, b])
            def _():
                dense[k, at(slot >> 2, TILE), at(slot & 3, TILE)] = tile
                dense_t[k, at(slot & 3, TILE), at(slot >> 2, TILE)] = tile.T


def block_body(p0, p1, p2, p3, block):
    me = place()
    for k, piece in enumerate((p0, p1, p2, p3)):
        block[at(me["z"] ^ k, PART), :] = piece[...]


def forward_body(dense, f0, f1, f2, f3, to1, to2, to3, own, total):
    me = place()
    total[...] = dot(dense[0], f0[...]) + dot(dense[1], f1[...]) + dot(dense[2], f2[...]) + dot(dense[3], f3[...])
    for k, to in enumerate((own, to1, to2, to3)):
        to[...] = total[at(me["x"] ^ k, PART), :]


def sum_body(own, r1, r2, r3, out):
    out[...] = own[...] + r1[...] + (r2[...] + r3[...])


def layer_body(mine, other, weight, cot, cot_other, output, message):
    me = place()
    aggregate = (mine[...] + other[...]).astype(BF)
    preact = dot(aggregate, weight[...])
    gates = jax.nn.sigmoid(preact)
    activation = (preact * gates).astype(BF)
    first = me["h"] == 0
    output[...] = jnp.where(first, activation[:SLICE], activation[SLICE:])
    a, b = cot[...], cot_other[...]
    cotangent = jnp.concatenate([jnp.where(first, a, b), jnp.where(first, b, a)], axis=0).astype(F32)
    message[0:PART, :] = aggregate
    message[PART:, :] = (cotangent * gates * (1.0 + preact * (1.0 - gates))).astype(BF)


def backward_body(dense_t, weight, m0, m1, m2, m3, to_c, aggregate, grad_pre, grad_agg):
    me = place()
    for k, m in enumerate((m0, m1, m2, m3)):
        rows = at(me["x"] ^ k, PART)
        aggregate[rows, :] = m[0:PART, :]
        grad_pre[rows, :] = m[PART:, :]
    grad = dot(grad_pre[...], weight[...], ((1,), (1,))).astype(BF)
    grad_agg[...] = grad
    to_c[0:BLOCK, :] = dot(dense_t[1], grad)
    to_c[BLOCK:, :] = dot(dense_t[3], grad)


def kept_body(dense_t, aggregate, grad_pre, grad_agg, keep, share, grad_w):
    me = place()
    grad_w[...] = dot(aggregate[...], grad_pre[...], ((0,), (0,)))
    share[...] = grad_w[at(me["x"], SLICE), :]
    grad = grad_agg[...]
    keep[0:BLOCK, :] = dot(dense_t[0], grad)
    keep[BLOCK:, :] = dot(dense_t[2], grad)


def after_c_body(keep, got, keep_w, got_w, to_u, own, own_w):
    own[...] = keep[0:BLOCK, :] + got[0:BLOCK, :]
    to_u[0:BLOCK, :] = (keep[BLOCK:, :] + got[BLOCK:, :]).astype(BF)
    share = keep_w[...] + got_w[...]
    put_split(to_u, BLOCK, share)
    own_w[...] = share


def after_u_body(own, own_w, got, to1, to2, to3, kept, kept_w, total):
    me = place()
    total[...] = own[...] + got[0:BLOCK, :].astype(F32)
    high, low = split(own_w[...])
    share = ((high.astype(F32) + low.astype(F32)) + get_split(got, BLOCK)).astype(BF)
    kept[...] = total[at(me["z"], PART), :]
    kept_w[...] = share
    for k, to in ((1, to1), (2, to2), (3, to3)):
        to[0:PART, :] = total[at(me["z"] ^ k, PART), :].astype(BF)
        to[PART:, :] = share


def after_z_body(kept, kept_w, r1, r2, r3, to_v):
    total = kept[...] + r1[0:PART, :].astype(F32)
    to_v[0:PART, :] = total + (r2[0:PART, :].astype(F32) + r3[0:PART, :].astype(F32))
    share = kept_w[...].astype(F32) + r1[PART:, :].astype(F32)
    to_v[PART:, :] = share + (r2[PART:, :].astype(F32) + r3[PART:, :].astype(F32))


def after_v_body(mine, got, piece, share):
    piece[...] = (mine[0:PART, :] + got[0:PART, :]).astype(BF)
    put_split(share, 0, mine[PART:, :] + got[PART:, :])


def finish_body(p0, p1, p2, p3, w0, w1, w2, w3, grad_features, grad_weight):
    me = place()
    for k, (piece, share) in enumerate(((p0, w0), (p1, w1), (p2, w2), (p3, w3))):
        grad_features[at(chunk_of(me, me["x"] ^ k), PART), :] = piece[...]
        grad_weight[at(me["x"] ^ k, SLICE), :] = get_split(share, 0)


def on_device(features, weight, cotangent, tile_values, tile_slots, tile_count):
    part = ((PART, WIDTH), BF)
    part32 = ((PART, WIDTH), F32)
    block = ((BLOCK, WIDTH), BF)
    share32 = ((SLICE, WIDTH), F32)
    dense_shape = ((4, BLOCK, BLOCK), BF)

    (chunk,) = call(chunk_body, [part], features, specs=[HBM], scratch=[pltpu.SemaphoreType.DMA])
    chunk = send(chunk, TO_COLUMN)
    cot_other = send(cotangent, FLIP_H)
    dense, dense_t = call(
        dense_body, [dense_shape, dense_shape], tile_slots, tile_count, tile_values, specs=[SMEM, SMEM, VMEM]
    )
    chunk, cot_other, dense, dense_t = lax.optimization_barrier((chunk, cot_other, dense, dense_t))
    (f0,) = call(block_body, [block], chunk, *[send(chunk, route) for route in FLIP_Z])
    f2 = send(f0, FLIP_U)
    f1 = send(f0, FLIP_C)
    f3 = send(f2, FLIP_C)
    *to, own = call(
        forward_body, [part32] * 4, dense, f0, f1, f2, f3, scratch=[pltpu.VMEM((BLOCK, WIDTH), F32)]
    )
    got = [send(value, route) for value, route in zip(to, FLIP_X)]
    (mine,) = call(sum_body, [part32], own, *got)
    other = send(mine, FLIP_H)
    output, message = call(
        layer_body, [((SLICE, WIDTH), BF), ((2 * PART, WIDTH), BF)], mine, other, weight, cotangent, cot_other
    )
    got = [send(message, route) for route in FLIP_X]
    to_c, aggregate, grad_pre, grad_agg = call(
        backward_body, [((2 * BLOCK, WIDTH), F32), block, block, block], dense_t, weight, message, *got
    )
    got = send(to_c, FLIP_C)
    keep, keep_w = call(
        kept_body, [((2 * BLOCK, WIDTH), F32), share32], dense_t, aggregate, grad_pre, grad_agg,
        scratch=[pltpu.VMEM((WIDTH, WIDTH), F32)],
    )
    got_w = send(keep_w, FLIP_C)
    to_u, own, own_w = call(
        after_c_body, [((BLOCK + 2 * SLICE, WIDTH), BF), ((BLOCK, WIDTH), F32), share32], keep, got, keep_w, got_w
    )
    got = send(to_u, FLIP_U)
    to_z = ((PART + SLICE, WIDTH), BF)
    *to, kept, kept_w = call(
        after_u_body, [to_z, to_z, to_z, part32, ((SLICE, WIDTH), BF)], own, own_w, got,
        scratch=[pltpu.VMEM((BLOCK, WIDTH), F32)],
    )
    got = [send(value, route) for value, route in zip(to, FLIP_Z)]
    (to_v,) = call(after_z_body, [((PART + SLICE, WIDTH), F32)], kept, kept_w, *got)
    got = send(to_v, FLIP_V)
    piece, share = call(after_v_body, [part, ((2 * SLICE, WIDTH), BF)], to_v, got)
    piece = send(piece, TO_ROW)
    shares = [share] + [send(share, route) for route in FLIP_X]
    pieces = [piece] + [send(piece, route) for route in FLIP_X]
    grad_features, grad_weight = call(
        finish_body, [((BLOCK, WIDTH), BF), ((WIDTH, WIDTH), F32)], *pieces, *shares
    )
    return output, grad_weight, grad_features


def solution(mesh):
    placed = (
        P("rows", None),
        P(),
        P(("rows", "rep"), None),
        P("rows", "rep", None, None, None),
        P("rows", "rep", None),
        P("rows", "rep"),
    )
    return jax.shard_map(
        on_device,
        mesh=mesh,
        in_specs=placed,
        out_specs=(P(("rows", "rep"), None), P(), P("rows", None)),
        check_vma=False,
    )
```

```python
import itertools

import jax
import jax.numpy as jnp
from jax import lax
from jax.experimental import pallas as pl
from jax.experimental.pallas import tpu as pltpu
from jax.sharding import PartitionSpec as P

BF = jnp.bfloat16
F32 = jnp.float32
TILE = 128
WIDTH = 256
BLOCK = 512
PART = 128
SLICE = 64
AXES = ("rows", "rep")


def u_of(y):
    return (y ^ (y >> 1)) & 1


def v_of(y):
    return y >> 1


Y_OF = {(u_of(y), v_of(y)): y for y in range(4)}
PLACES = list(itertools.product(range(4), range(4), range(2), range(4), range(2)))


def index_of(z, y, c, x, h):
    return (z * 8 + y * 2 + c) * 8 + x * 2 + h


def pairs(target):
    return [(index_of(*place), index_of(*target(*place))) for place in PLACES]


FLIP_C = pairs(lambda z, y, c, x, h: (z, y, 1 - c, x, h))
FLIP_U = pairs(lambda z, y, c, x, h: (z, Y_OF[1 - u_of(y), v_of(y)], c, x, h))
FLIP_V = pairs(lambda z, y, c, x, h: (z, Y_OF[u_of(y), 1 - v_of(y)], c, x, h))
FLIP_H = pairs(lambda z, y, c, x, h: (z, y, c, x, 1 - h))
FLIP_X = [pairs(lambda z, y, c, x, h, k=k: (z, y, c, x ^ k, h)) for k in (1, 2, 3)]
FLIP_Z = [pairs(lambda z, y, c, x, h, k=k: (z ^ k, y, c, x, h)) for k in (1, 2, 3)]
ROUTE = (((2, 1, 3, 0), (0, 3, 2, 1), (2, 1, 0, 3), (3, 0, 2, 1)), ((0, 1, 3, 2), (0, 1, 2, 3), (0, 1, 2, 3), (1, 0, 2, 3)))
TO_ROW = pairs(lambda z, y, c, x, h: (x, Y_OF[u_of(y), h], c, ROUTE[v_of(y) == h][x][z], 1 - v_of(y)))
TO_COLUMN = [(there, here) for here, there in TO_ROW]


def chunk_table(same):
    word = sum((z << (8 * x + 2 * ROUTE[same][x][z])) for x in range(4) for z in range(4))
    return word - (1 << 32) if word >> 31 else word


CHUNKS = (chunk_table(0), chunk_table(1))


def send(value, route):
    return lax.ppermute(value, AXES, route)


def place():
    r = lax.axis_index("rows")
    p = lax.axis_index("rep")
    y = (r >> 1) & 3
    v = y >> 1
    return dict(z=r >> 3, c=r & 1, u=(y ^ v) & 1, v=v, x=p >> 1, h=p & 1)


def chunk_of(me, x):
    word = jnp.where((1 - me["h"]) == me["v"], jnp.int32(CHUNKS[1]), jnp.int32(CHUNKS[0]))
    return (word >> (8 * me["z"] + 2 * x)) & 3


def at(index, size):
    return pl.ds(pl.multiple_of(index * size, size), size)


def dot(a, b, dims=((1,), (0,))):
    return lax.dot_general(a, b, (dims, ((), ())), preferred_element_type=F32)


SMEM = pl.BlockSpec(memory_space=pltpu.SMEM)
VMEM = pl.BlockSpec(memory_space=pltpu.VMEM)
HBM = pl.BlockSpec(memory_space=pl.ANY)


def call(body, outs, *args, specs=None, scratch=()):
    return pl.pallas_call(
        body,
        out_shape=[jax.ShapeDtypeStruct(shape, dtype) for shape, dtype in outs],
        in_specs=specs or [VMEM] * len(args),
        out_specs=[VMEM] * len(outs),
        scratch_shapes=list(scratch),
        compiler_params=pltpu.CompilerParams(vmem_limit_bytes=24 * 2**20),
    )(*args)


def split(value):
    high = value.astype(BF)
    return high, (value - high.astype(F32)).astype(BF)


def put_split(ref, start, value):
    high, low = split(value)
    ref[start : start + SLICE, :] = high
    ref[start + SLICE : start + 2 * SLICE, :] = low


def get_split(ref, start):
    return ref[start : start + SLICE, :].astype(F32) + ref[start + SLICE : start + 2 * SLICE, :].astype(F32)


def chunk_body(features, out, sem):
    me = place()
    copy = pltpu.make_async_copy(features.at[at(chunk_of(me, me["x"]), PART), :], out, sem)
    copy.start()
    copy.wait()


def dense_body(slots, count, tiles, dense, dense_t):
    me = place()
    dense[...] = jnp.zeros_like(dense)
    dense_t[...] = jnp.zeros_like(dense_t)
    for k in range(4):
        b = ((me["u"] ^ me["h"]) * 2 + me["c"]) ^ k
        for s in range(2):
            slot = slots[0, b, s]
            tile = jnp.where(s < count[0, b], tiles[0, b, s], jnp.zeros((), BF))

            @pl.when(s < count[0, b])
            def _():
                dense[k, at(slot >> 2, TILE), at(slot & 3, TILE)] = tile
                dense_t[k, at(slot & 3, TILE), at(slot >> 2, TILE)] = tile.T


def block_body(p0, p1, p2, p3, block):
    me = place()
    for k, piece in enumerate((p0, p1, p2, p3)):
        block[at(me["z"] ^ k, PART), :] = piece[...]


def forward_body(dense, f0, f1, f2, f3, to3, to2, to1, own, total):
    me = place()
    total[...] = dot(dense[0], f0[...]) + dot(dense[1], f1[...]) + dot(dense[2], f2[...]) + dot(dense[3], f3[...])
    for k, to in enumerate((own, to1, to2, to3)):
        to[...] = total[at(me["x"] ^ k, PART), :]


def sum_body(own, r3, r2, r1, cot, to_h):
    total = own[...] + r1[...] + (r2[...] + r3[...])
    high, low = split(total)
    to_h[0:PART, :] = high
    to_h[PART : 2 * PART, :] = low
    to_h[2 * PART :, :] = cot[...]


def layer_body(mine, got, weight, output, message):
    me = place()
    parts = [ref[0:PART, :].astype(F32) + ref[PART : 2 * PART, :].astype(F32) for ref in (mine, got)]
    aggregate = (parts[0] + parts[1]).astype(BF)
    preact = dot(aggregate, weight[...])
    gates = jax.nn.sigmoid(preact)
    activation = (preact * gates).astype(BF)
    first = me["h"] == 0
    output[...] = jnp.where(first, activation[:SLICE], activation[SLICE:])
    a, b = mine[2 * PART :, :], got[2 * PART :, :]
    cotangent = jnp.concatenate([jnp.where(first, a, b), jnp.where(first, b, a)], axis=0).astype(F32)
    message[0:PART, :] = aggregate
    message[PART:, :] = (cotangent * gates * (1.0 + preact * (1.0 - gates))).astype(BF)


def backward_body(dense_t, weight, m0, m1, m2, m3, to_c, aggregate, grad_pre, grad_agg):
    me = place()
    for k, m in enumerate((m0, m1, m2, m3)):
        rows = at(me["x"] ^ k, PART)
        aggregate[rows, :] = m[0:PART, :]
        grad_pre[rows, :] = m[PART:, :]
    grad = dot(grad_pre[...], weight[...], ((1,), (1,))).astype(BF)
    grad_agg[...] = grad
    to_c[...] = dot(dense_t[3], grad)


def kept_body(dense_t, aggregate, grad_pre, grad_agg, to_c, keep_other, keep, share, grad_w):
    me = place()
    grad = grad_agg[...]
    to_c[...] = dot(dense_t[1], grad)
    keep_other[...] = dot(dense_t[2], grad)
    keep[...] = dot(dense_t[0], grad)
    grad_w[...] = dot(aggregate[...], grad_pre[...], ((0,), (0,)))
    share[...] = grad_w[at(me["x"], SLICE), :]


def to_u_body(keep, got, to3, to2, to1, to0):
    me = place()
    for k, to in ((3, to3), (2, to2), (1, to1), (0, to0)):
        rows = at(me["z"] ^ k, PART)
        to[...] = (keep[rows, :] + got[rows, :]).astype(BF)


def after_c_body(keep, got, keep_w, got_w, s3, s2, s1, s0, share):
    me = place()
    for k, part in ((3, s3), (2, s2), (1, s1), (0, s0)):
        rows = at(me["z"] ^ k, PART)
        part[...] = keep[rows, :] + got[rows, :]
    share[...] = (keep_w[...] + got_w[...]).astype(BF)


def to_z_body(own, got, share, to):
    to[0:PART, :] = (own[...] + got[...].astype(F32)).astype(BF)
    to[PART:, :] = share[...]


def after_z_body(own, got, share, r3, r2, r1, to_v, share_z):
    total = own[...] + got[...].astype(F32) + r1[0:PART, :].astype(F32)
    to_v[...] = total + (r2[0:PART, :].astype(F32) + r3[0:PART, :].astype(F32))
    pair = share[...].astype(F32) + r1[PART:, :].astype(F32)
    share_z[...] = pair + (r2[PART:, :].astype(F32) + r3[PART:, :].astype(F32))


def after_v_body(mine, got, piece):
    piece[...] = (mine[...] + got[...]).astype(BF)


def add_body(mine, got, total):
    total[...] = mine[...] + got[...]


def last_body(piece, mine, got, message):
    message[0:PART, :] = piece[...]
    put_split(message, PART, mine[...] + got[...])


def finish_body(m0, m1, m2, m3, grad_features, grad_weight):
    me = place()
    for k, message in enumerate((m0, m1, m2, m3)):
        grad_features[at(chunk_of(me, me["x"] ^ k), PART), :] = message[0:PART, :]
        grad_weight[at(me["x"] ^ k, SLICE), :] = get_split(message, PART)


def on_device(features, weight, cotangent, tile_values, tile_slots, tile_count):
    part = ((PART, WIDTH), BF)
    part32 = ((PART, WIDTH), F32)
    block = ((BLOCK, WIDTH), BF)
    block32 = ((BLOCK, WIDTH), F32)
    share32 = ((SLICE, WIDTH), F32)
    dense_shape = ((4, BLOCK, BLOCK), BF)

    (chunk,) = call(chunk_body, [part], features, specs=[HBM], scratch=[pltpu.SemaphoreType.DMA])
    chunk = send(chunk, TO_COLUMN)
    dense, dense_t = call(
        dense_body, [dense_shape, dense_shape], tile_slots, tile_count, tile_values, specs=[SMEM, SMEM, VMEM]
    )
    chunk, dense, dense_t = lax.optimization_barrier((chunk, dense, dense_t))
    chunks = [chunk] + [send(chunk, route) for route in FLIP_Z]
    others = [send(value, FLIP_U) for value in chunks]
    (f0,) = call(block_body, [block], *chunks)
    f1 = send(f0, FLIP_C)
    (f2,) = call(block_body, [block], *others)
    f3 = send(f2, FLIP_C)
    to3, to2, to1, own = call(
        forward_body, [part32] * 4, dense, f0, f1, f2, f3, scratch=[pltpu.VMEM((BLOCK, WIDTH), F32)]
    )
    got = [send(value, route) for value, route in zip((to3, to2, to1), FLIP_X[::-1])]
    (mine,) = call(sum_body, [((2 * PART + SLICE, WIDTH), BF)], own, *got, cotangent)
    got = send(mine, FLIP_H)
    output, message = call(
        layer_body, [((SLICE, WIDTH), BF), ((2 * PART, WIDTH), BF)], mine, got, weight
    )
    got = [send(message, route) for route in FLIP_X]

    to_c, aggregate, grad_pre, grad_agg = call(
        backward_body, [block32, block, block, block], dense_t, weight, message, *got
    )
    got_other = send(to_c, FLIP_C)
    to_c, keep_other, keep, share = call(
        kept_body, [block32, block32, block32, share32], dense_t, aggregate, grad_pre, grad_agg,
        scratch=[pltpu.VMEM((WIDTH, WIDTH), F32)],
    )
    got = send(to_c, FLIP_C)
    got_w = send(share, FLIP_C)
    to_u = call(to_u_body, [part] * 4, keep_other, got_other)
    from_u = [send(value, FLIP_U) for value in to_u]
    *owns, share = call(after_c_body, [part32] * 4 + [((SLICE, WIDTH), BF)], keep, got, share, got_w)
    from_z = []
    for own, got, route in zip(owns, from_u, FLIP_Z[::-1]):
        (to_z,) = call(to_z_body, [((PART + SLICE, WIDTH), BF)], own, got, share)
        from_z.append(send(to_z, route))
    to_v, share = call(after_z_body, [part32, share32], owns[3], from_u[3], share, *from_z)
    got = send(to_v, FLIP_V)
    got_w = send(share, FLIP_U)
    (piece,) = call(after_v_body, [part], to_v, got)
    (share,) = call(add_body, [share32], share, got_w)
    piece = send(piece, TO_ROW)
    got_w = send(share, FLIP_V)
    (message,) = call(last_body, [((PART + 2 * SLICE, WIDTH), BF)], piece, share, got_w)
    messages = [message] + [send(message, route) for route in FLIP_X]
    grad_features, grad_weight = call(finish_body, [block, ((WIDTH, WIDTH), F32)], *messages)
    return output, grad_weight, grad_features


def solution(mesh):
    placed = (
        P("rows", None),
        P(),
        P(("rows", "rep"), None),
        P("rows", "rep", None, None, None),
        P("rows", "rep", None),
        P("rows", "rep"),
    )
    return jax.shard_map(
        on_device,
        mesh=mesh,
        in_specs=placed,
        out_specs=(P(("rows", "rep"), None), P(), P("rows", None)),
        check_vma=False,
    )
```

```python
import itertools

import jax
import jax.numpy as jnp
from jax import lax
from jax.experimental import pallas as pl
from jax.experimental.pallas import tpu as pltpu
from jax.sharding import PartitionSpec as P

BF = jnp.bfloat16
F32 = jnp.float32
TILE = 128
WIDTH = 256
BLOCK = 512
PART = 128
SLICE = 64
AXES = ("rows", "rep")


def u_of(y):
    return (y ^ (y >> 1)) & 1


def v_of(y):
    return y >> 1


Y_OF = {(u_of(y), v_of(y)): y for y in range(4)}
PLACES = list(itertools.product(range(4), range(4), range(2), range(4), range(2)))


def index_of(z, y, c, x, h):
    return (z * 8 + y * 2 + c) * 8 + x * 2 + h


def pairs(target):
    return [(index_of(*place), index_of(*target(*place))) for place in PLACES]


FLIP_C = pairs(lambda z, y, c, x, h: (z, y, 1 - c, x, h))
FLIP_U = pairs(lambda z, y, c, x, h: (z, Y_OF[1 - u_of(y), v_of(y)], c, x, h))
FLIP_V = pairs(lambda z, y, c, x, h: (z, Y_OF[u_of(y), 1 - v_of(y)], c, x, h))
FLIP_H = pairs(lambda z, y, c, x, h: (z, y, c, x, 1 - h))
FLIP_X = [pairs(lambda z, y, c, x, h, k=k: (z, y, c, x ^ k, h)) for k in (1, 2, 3)]
FLIP_Z = [pairs(lambda z, y, c, x, h, k=k: (z ^ k, y, c, x, h)) for k in (1, 2, 3)]
ROUTE = (((2, 1, 3, 0), (0, 3, 2, 1), (2, 1, 0, 3), (3, 0, 2, 1)), ((0, 1, 3, 2), (0, 1, 2, 3), (0, 1, 2, 3), (1, 0, 2, 3)))
TO_ROW = pairs(lambda z, y, c, x, h: (x, Y_OF[u_of(y), h], c, ROUTE[v_of(y) == h][x][z], 1 - v_of(y)))
TO_COLUMN = [(there, here) for here, there in TO_ROW]


def chunk_table(same):
    word = sum((z << (8 * x + 2 * ROUTE[same][x][z])) for x in range(4) for z in range(4))
    return word - (1 << 32) if word >> 31 else word


CHUNKS = (chunk_table(0), chunk_table(1))


def send(value, route):
    return lax.ppermute(value, AXES, route)


def place():
    r = lax.axis_index("rows")
    p = lax.axis_index("rep")
    y = (r >> 1) & 3
    v = y >> 1
    return dict(z=r >> 3, c=r & 1, u=(y ^ v) & 1, v=v, x=p >> 1, h=p & 1)


def chunk_of(me, x):
    word = jnp.where((1 - me["h"]) == me["v"], jnp.int32(CHUNKS[1]), jnp.int32(CHUNKS[0]))
    return (word >> (8 * me["z"] + 2 * x)) & 3


def at(index, size):
    return pl.ds(pl.multiple_of(index * size, size), size)


def dot(a, b, dims=((1,), (0,))):
    return lax.dot_general(a, b, (dims, ((), ())), preferred_element_type=F32)


SMEM = pl.BlockSpec(memory_space=pltpu.SMEM)
VMEM = pl.BlockSpec(memory_space=pltpu.VMEM)
HBM = pl.BlockSpec(memory_space=pl.ANY)


def call(body, outs, *args, specs=None, scratch=()):
    return pl.pallas_call(
        body,
        out_shape=[jax.ShapeDtypeStruct(shape, dtype) for shape, dtype in outs],
        in_specs=specs or [VMEM] * len(args),
        out_specs=[VMEM] * len(outs),
        scratch_shapes=list(scratch),
        compiler_params=pltpu.CompilerParams(vmem_limit_bytes=24 * 2**20),
    )(*args)


def split(value):
    high = value.astype(BF)
    return high, (value - high.astype(F32)).astype(BF)


def put_split(ref, start, value):
    high, low = split(value)
    ref[start : start + SLICE, :] = high
    ref[start + SLICE : start + 2 * SLICE, :] = low


def get_split(ref, start):
    return ref[start : start + SLICE, :].astype(F32) + ref[start + SLICE : start + 2 * SLICE, :].astype(F32)


def chunk_body(features, out, sem):
    me = place()
    copy = pltpu.make_async_copy(features.at[at(chunk_of(me, me["x"]), PART), :], out, sem)
    copy.start()
    copy.wait()


def dense_body(slots, count, tiles, dense, dense_t):
    me = place()
    dense[...] = jnp.zeros_like(dense)
    dense_t[...] = jnp.zeros_like(dense_t)
    for k in range(4):
        b = ((me["u"] ^ me["h"]) * 2 + me["c"]) ^ k
        for s in range(2):
            slot = slots[0, b, s]
            tile = jnp.where(s < count[0, b], tiles[0, b, s], jnp.zeros((), BF))

            @pl.when(s < count[0, b])
            def _():
                dense[k, at(slot >> 2, TILE), at(slot & 3, TILE)] = tile
                dense_t[k, at(slot & 3, TILE), at(slot >> 2, TILE)] = tile.T


def pair_body(low, high, out):
    out[0:PART, :] = low[...]
    out[PART:, :] = high[...]


def forward_body(dense, a0, b0, a1, b1, a2, b2, a3, b3, to3, to2, to1, own, blocks, total):
    me = place()
    for i, (first, second) in enumerate(((a0, b0), (a1, b1), (a2, b2), (a3, b3))):
        for k, part in ((3, first[0:PART, :]), (0, first[PART:, :]), (2, second[0:PART, :]), (1, second[PART:, :])):
            blocks[i, at(me["z"] ^ k, PART), :] = part
    total[...] = dot(dense[0], blocks[0]) + dot(dense[1], blocks[1]) + (dot(dense[2], blocks[2]) + dot(dense[3], blocks[3]))
    for k, to in enumerate((own, to1, to2, to3)):
        to[...] = total[at(me["x"] ^ k, PART), :]


def sum_body(own, r3, r2, r1, cot, to_h):
    total = own[...] + r1[...] + (r2[...] + r3[...])
    high, low = split(total)
    to_h[0:PART, :] = high
    to_h[PART : 2 * PART, :] = low
    to_h[2 * PART :, :] = cot[...]


def layer_body(mine, got, weight, output, message):
    me = place()
    parts = [ref[0:PART, :].astype(F32) + ref[PART : 2 * PART, :].astype(F32) for ref in (mine, got)]
    aggregate = (parts[0] + parts[1]).astype(BF)
    preact = dot(aggregate, weight[...])
    gates = jax.nn.sigmoid(preact)
    activation = (preact * gates).astype(BF)
    first = me["h"] == 0
    output[...] = jnp.where(first, activation[:SLICE], activation[SLICE:])
    a, b = mine[2 * PART :, :], got[2 * PART :, :]
    cotangent = jnp.concatenate([jnp.where(first, a, b), jnp.where(first, b, a)], axis=0).astype(F32)
    message[0:PART, :] = aggregate
    message[PART:, :] = (cotangent * gates * (1.0 + preact * (1.0 - gates))).astype(BF)


def backward_body(dense_t, weight, m0, m1, m2, m3, to_c, aggregate, grad_pre, grad_agg):
    me = place()
    for k, m in enumerate((m0, m1, m2, m3)):
        rows = at(me["x"] ^ k, PART)
        aggregate[rows, :] = m[0:PART, :]
        grad_pre[rows, :] = m[PART:, :]
    grad = dot(grad_pre[...], weight[...], ((1,), (1,))).astype(BF)
    grad_agg[...] = grad
    to_c[...] = dot(dense_t[3], grad)


def share_body(dense_t, aggregate, grad_pre, grad_agg, keep, share, grad_w):
    me = place()
    keep[...] = dot(dense_t[2], grad_agg[...])
    grad_w[...] = dot(aggregate[...], grad_pre[...], ((0,), (0,)))
    share[...] = grad_w[at(me["x"], SLICE), :].astype(BF)


def to_u_body(keep, got, share, first, second):
    me = place()
    for k, out, start in ((3, first, 0), (2, first, PART), (1, second, 0), (0, second, PART)):
        rows = at(me["z"] ^ k, PART)
        out[start : start + PART, :] = (keep[rows, :] + got[rows, :]).astype(BF)
    first[2 * PART :, :] = share[...]


def kept_body(dense_t, grad_agg, to_c, keep):
    to_c[...] = dot(dense_t[1], grad_agg[...])
    keep[...] = dot(dense_t[0], grad_agg[...])


def after_c_body(keep, got, own, total):
    me = place()
    total[...] = keep[...] + got[...]
    for k in range(4):
        own[k * PART : (k + 1) * PART, :] = total[at(me["z"] ^ k, PART), :]


def to_z_body(own, got, share, to3, to2):
    pair = (share[...].astype(F32) + got[2 * PART :, :].astype(F32)).astype(BF)
    for to, start, k in ((to3, 0, 3), (to2, PART, 2)):
        to[0:PART, :] = (own[k * PART : (k + 1) * PART, :] + got[start : start + PART, :].astype(F32)).astype(BF)
        to[PART:, :] = pair


def to_z1_body(own, got, share, got_first, to, kept_share):
    to[0:PART, :] = (own[PART : 2 * PART, :] + got[0:PART, :].astype(F32)).astype(BF)
    pair = (share[...].astype(F32) + got_first[2 * PART :, :].astype(F32)).astype(BF)
    to[PART:, :] = pair
    kept_share[...] = pair


def after_z_body(own, got, share, r3, r2, r1, to_v):
    total = own[0:PART, :] + got[PART:, :].astype(F32) + r1[0:PART, :].astype(F32)
    to_v[0:PART, :] = total + (r2[0:PART, :].astype(F32) + r3[0:PART, :].astype(F32))
    pair = share[...].astype(F32) + r1[PART:, :].astype(F32)
    to_v[PART:, :] = pair + (r2[PART:, :].astype(F32) + r3[PART:, :].astype(F32))


def after_v_body(mine, got, piece, share):
    piece[...] = (mine[0:PART, :] + got[0:PART, :]).astype(BF)
    share[...] = mine[PART:, :] + got[PART:, :]


def last_share_body(mine, got, message):
    put_split(message, 0, mine[...] + got[...])


def finish_body(p0, p1, p2, p3, w0, w1, w2, w3, grad_features, grad_weight):
    me = place()
    for k, (piece, share) in enumerate(((p0, w0), (p1, w1), (p2, w2), (p3, w3))):
        grad_features[at(chunk_of(me, me["x"] ^ k), PART), :] = piece[...]
        grad_weight[at(me["x"] ^ k, SLICE), :] = get_split(share, 0)


def on_device(features, weight, cotangent, tile_values, tile_slots, tile_count):
    part = ((PART, WIDTH), BF)
    part32 = ((PART, WIDTH), F32)
    block = ((BLOCK, WIDTH), BF)
    block32 = ((BLOCK, WIDTH), F32)
    share32 = ((SLICE, WIDTH), F32)
    share16 = ((SLICE, WIDTH), BF)
    two = ((2 * PART, WIDTH), BF)
    dense_shape = ((4, BLOCK, BLOCK), BF)

    (chunk,) = call(chunk_body, [part], features, specs=[HBM], scratch=[pltpu.SemaphoreType.DMA])
    chunk = send(chunk, TO_COLUMN)
    dense, dense_t = call(
        dense_body, [dense_shape, dense_shape], tile_slots, tile_count, tile_values, specs=[SMEM, SMEM, VMEM]
    )
    chunk, dense, dense_t = lax.optimization_barrier((chunk, dense, dense_t))
    chunks = [chunk] + [send(chunk, route) for route in FLIP_Z]
    c0, c1, c2, c3 = chunks
    mine = [call(pair_body, [two], c3, c0)[0], call(pair_body, [two], c2, c1)[0]]
    by_u = [send(value, FLIP_U) for value in mine]
    by_c = [send(value, FLIP_C) for value in mine]
    by_uc = [send(value, FLIP_C) for value in by_u]
    to3, to2, to1, own = call(
        forward_body, [part32] * 4, dense, *mine, *by_c, *by_u, *by_uc,
        scratch=[pltpu.VMEM((4, BLOCK, WIDTH), BF), pltpu.VMEM((BLOCK, WIDTH), F32)],
    )
    got = [send(value, route) for value, route in zip((to3, to2, to1), FLIP_X[::-1])]
    (mine,) = call(sum_body, [((2 * PART + SLICE, WIDTH), BF)], own, *got, cotangent)
    got = send(mine, FLIP_H)
    output, message = call(
        layer_body, [((SLICE, WIDTH), BF), ((2 * PART, WIDTH), BF)], mine, got, weight
    )
    got = [send(message, route) for route in FLIP_X]

    to_c, aggregate, grad_pre, grad_agg = call(
        backward_body, [block32, block, block, block], dense_t, weight, message, *got
    )
    got = send(to_c, FLIP_C)
    keep, share = call(
        share_body, [block32, share16], dense_t, aggregate, grad_pre, grad_agg,
        scratch=[pltpu.VMEM((WIDTH, WIDTH), F32)],
    )
    first, second = call(to_u_body, [((2 * PART + SLICE, WIDTH), BF), two], keep, got, share)
    got_first, got_second = send(first, FLIP_U), send(second, FLIP_U)
    to_c, keep = call(kept_body, [block32, block32], dense_t, grad_agg)
    (own,) = call(after_c_body, [block32], keep, send(to_c, FLIP_C), scratch=[pltpu.VMEM((BLOCK, WIDTH), F32)])
    to_z = ((PART + SLICE, WIDTH), BF)
    to3, to2 = call(to_z_body, [to_z, to_z], own, got_first, share)
    to1, share = call(to_z1_body, [to_z, share16], own, got_second, share, got_first)
    from_z = [send(value, route) for value, route in zip((to3, to2, to1), FLIP_Z[::-1])]
    (to_v,) = call(after_z_body, [((PART + SLICE, WIDTH), F32)], own, got_second, share, *from_z)
    piece, share = call(after_v_body, [part, share32], to_v, send(to_v, FLIP_V))
    piece = send(piece, TO_ROW)
    (share,) = call(last_share_body, [((2 * SLICE, WIDTH), BF)], share, send(share, FLIP_C))
    shares = [share] + [send(share, route) for route in FLIP_X]
    piece, *shares = lax.optimization_barrier((piece, *shares))
    pieces = [piece] + [send(piece, route) for route in FLIP_X]
    grad_features, grad_weight = call(finish_body, [block, ((WIDTH, WIDTH), F32)], *pieces, *shares)
    return output, grad_weight, grad_features


def solution(mesh):
    placed = (
        P("rows", None),
        P(),
        P(("rows", "rep"), None),
        P("rows", "rep", None, None, None),
        P("rows", "rep", None),
        P("rows", "rep"),
    )
    return jax.shard_map(
        on_device,
        mesh=mesh,
        in_specs=placed,
        out_specs=(P(("rows", "rep"), None), P(), P("rows", None)),
        check_vma=False,
    )
```

```python
import functools
import itertools

import jax
import jax.numpy as jnp
from jax import lax
from jax.experimental import pallas as pl
from jax.experimental.pallas import tpu as pltpu
from jax.sharding import PartitionSpec as P

BF = jnp.bfloat16
F32 = jnp.float32
TILE = 128
WIDTH = 256
BLOCK = 512
PART = 128
SLICE = 64
AXES = ("rows", "rep")


def u_of(y):
    return (y ^ (y >> 1)) & 1


def v_of(y):
    return y >> 1


Y_OF = {(u_of(y), v_of(y)): y for y in range(4)}
PLACES = list(itertools.product(range(4), range(4), range(2), range(4), range(2)))


def index_of(z, y, c, x, h):
    return (z * 8 + y * 2 + c) * 8 + x * 2 + h


def pairs(target):
    return [(index_of(*place), index_of(*target(*place))) for place in PLACES]


FLIP_C = pairs(lambda z, y, c, x, h: (z, y, 1 - c, x, h))
FLIP_U = pairs(lambda z, y, c, x, h: (z, Y_OF[1 - u_of(y), v_of(y)], c, x, h))
FLIP_V = pairs(lambda z, y, c, x, h: (z, Y_OF[u_of(y), 1 - v_of(y)], c, x, h))
FLIP_H = pairs(lambda z, y, c, x, h: (z, y, c, x, 1 - h))
FLIP_X = [pairs(lambda z, y, c, x, h, k=k: (z, y, c, x ^ k, h)) for k in (1, 2, 3)]
FLIP_Z = [pairs(lambda z, y, c, x, h, k=k: (z ^ k, y, c, x, h)) for k in (1, 2, 3)]
ROUTE = (((2, 1, 3, 0), (0, 3, 2, 1), (2, 1, 0, 3), (3, 0, 2, 1)), ((0, 1, 3, 2), (0, 1, 2, 3), (0, 1, 2, 3), (1, 0, 2, 3)))
TO_ROW = pairs(lambda z, y, c, x, h: (x, Y_OF[u_of(y), h], c, ROUTE[v_of(y) == h][x][z], 1 - v_of(y)))
TO_COLUMN = [(there, here) for here, there in TO_ROW]


def chunk_table(same):
    word = sum((z << (8 * x + 2 * ROUTE[same][x][z])) for x in range(4) for z in range(4))
    return word - (1 << 32) if word >> 31 else word


CHUNKS = (chunk_table(0), chunk_table(1))


def send(value, route):
    return lax.ppermute(value, AXES, route)


def spread(value, routes):
    return [value] + [send(value, route) for route in routes[::-1]]


def place():
    r = lax.axis_index("rows")
    p = lax.axis_index("rep")
    y = (r >> 1) & 3
    v = y >> 1
    return dict(z=r >> 3, c=r & 1, u=(y ^ v) & 1, v=v, x=p >> 1, h=p & 1)


def chunk_of(me, x):
    word = jnp.where((1 - me["h"]) == me["v"], jnp.int32(CHUNKS[1]), jnp.int32(CHUNKS[0]))
    return (word >> (8 * me["z"] + 2 * x)) & 3


def at(index, size):
    return pl.ds(pl.multiple_of(index * size, size), size)


def dot(a, b, dims=((1,), (0,))):
    return lax.dot_general(a, b, (dims, ((), ())), preferred_element_type=F32)


SMEM = pl.BlockSpec(memory_space=pltpu.SMEM)
VMEM = pl.BlockSpec(memory_space=pltpu.VMEM)
HBM = pl.BlockSpec(memory_space=pl.ANY)


def call(body, outs, *args, specs=None, scratch=()):
    return pl.pallas_call(
        body,
        out_shape=[jax.ShapeDtypeStruct(shape, dtype) for shape, dtype in outs],
        in_specs=specs or [VMEM] * len(args),
        out_specs=[VMEM] * len(outs),
        scratch_shapes=list(scratch),
        compiler_params=pltpu.CompilerParams(vmem_limit_bytes=24 * 2**20),
    )(*args)


def split(value):
    high = value.astype(BF)
    return high, (value - high.astype(F32)).astype(BF)


def put_split(ref, start, value):
    high, low = split(value)
    ref[start : start + SLICE, :] = high
    ref[start + SLICE : start + 2 * SLICE, :] = low


def get_split(ref, start):
    return ref[start : start + SLICE, :].astype(F32) + ref[start + SLICE : start + 2 * SLICE, :].astype(F32)


def chunk_body(features, out, sem):
    me = place()
    copy = pltpu.make_async_copy(features.at[at(chunk_of(me, me["x"]), PART), :], out, sem)
    copy.start()
    copy.wait()


def dense_body(slots, count, tiles, dense, dense_t):
    me = place()
    dense[...] = jnp.zeros_like(dense)
    dense_t[...] = jnp.zeros_like(dense_t)
    for k in range(4):
        b = ((me["u"] ^ me["h"]) * 2 + me["c"]) ^ k
        for s in range(2):
            slot = slots[0, b, s]
            tile = jnp.where(s < count[0, b], tiles[0, b, s], jnp.zeros((), BF))

            @pl.when(s < count[0, b])
            def _():
                dense[k, at(slot >> 2, TILE), at(slot & 3, TILE)] = tile
                dense_t[k, at(slot & 3, TILE), at(slot >> 2, TILE)] = tile.T


def pair_body(low, high, out):
    out[0:PART, :] = low[...]
    out[PART:, :] = high[...]


def put_block(me, blocks, i, first, second):
    for k, part in ((3, first[0:PART, :]), (0, first[PART:, :]), (2, second[0:PART, :]), (1, second[PART:, :])):
        blocks[i, at(me["z"] ^ k, PART), :] = part


def forward_body(dense, b0, a0, b1, a1, b2, a2, total, blocks):
    me = place()
    for i, (first, second) in enumerate(((a0, b0), (a1, b1), (a2, b2))):
        put_block(me, blocks, i, first, second)
    total[...] = dot(dense[0], blocks[0]) + dot(dense[1], blocks[1]) + dot(dense[2], blocks[2])


def forward_last_body(dense, b3, a3, most, to3, to2, to1, own, blocks, total):
    me = place()
    put_block(me, blocks, 0, a3, b3)
    total[...] = most[...] + dot(dense[3], blocks[0])
    for k, to in enumerate((own, to1, to2, to3)):
        to[...] = total[at(me["x"] ^ k, PART), :]


def sum_body(own, r3, r2, r1, cot, to_h):
    total = own[...] + r1[...] + (r2[...] + r3[...])
    high, low = split(total)
    to_h[0:PART, :] = high
    to_h[PART : 2 * PART, :] = low
    to_h[2 * PART :, :] = cot[...]


def aggregate_of(mine, got):
    parts = [ref[0:PART, :].astype(F32) + ref[PART : 2 * PART, :].astype(F32) for ref in (mine, got)]
    return (parts[0] + parts[1]).astype(BF)


def layer_body(mine, got, weight, message):
    aggregate = aggregate_of(mine, got)
    preact = dot(aggregate, weight[...])
    gates = jax.nn.sigmoid(preact)
    first = place()["h"] == 0
    a, b = mine[2 * PART :, :], got[2 * PART :, :]
    cotangent = jnp.concatenate([jnp.where(first, a, b), jnp.where(first, b, a)], axis=0).astype(F32)
    message[0:PART, :] = aggregate
    message[PART:, :] = (cotangent * gates * (1.0 + preact * (1.0 - gates))).astype(BF)


def output_body(message, weight, output):
    own = message[at(place()["h"], SLICE), :]
    preact = dot(own, weight[...])
    output[...] = (preact * jax.nn.sigmoid(preact)).astype(BF)


def backward_body(dense_t, weight, m0, m3, m2, m1, to_c, grad_agg, aggregate, grad_pre, grad_w):
    me = place()
    for k, m in enumerate((m0, m1, m2, m3)):
        rows = at(me["x"] ^ k, PART)
        aggregate[rows, :] = m[0:PART, :]
        grad_pre[rows, :] = m[PART:, :]
    grad = dot(grad_pre[...], weight[...], ((1,), (1,))).astype(BF)
    grad_agg[...] = grad
    to_c[0:BLOCK, :] = dot(dense_t[3], grad)
    grad_w[...] = dot(aggregate[...], grad_pre[...], ((0,), (0,)))
    to_c[BLOCK:, :] = grad_w[at(me["x"], SLICE), :]


def keep_body(dense_t, grad_agg, keep):
    keep[...] = dot(dense_t[2], grad_agg[...])


def to_u_body(keep, mine, got, u3, u2, u1, u0, share):
    me = place()
    for k, out in ((3, u3), (2, u2), (1, u1), (0, u0)):
        rows = at(me["z"] ^ k, PART)
        out[0:PART, :] = (keep[rows, :] + got[rows, :]).astype(BF)
    both = (mine[BLOCK:, :] + got[BLOCK:, :]).astype(BF)
    u3[PART:, :] = both
    share[...] = both


def kept_body(dense_t, grad_agg, to_c, keep):
    to_c[...] = dot(dense_t[1], grad_agg[...])
    keep[...] = dot(dense_t[0], grad_agg[...])


def after_c_body(keep, got, own, total):
    me = place()
    total[...] = keep[...] + got[...]
    for k in range(4):
        own[k * PART : (k + 1) * PART, :] = total[at(me["z"] ^ k, PART), :]


def pair_share(share, got_first):
    return (share[...].astype(F32) + got_first[PART:, :].astype(F32)).astype(BF)


def to_z_body(k, own, got, share, got_first, to):
    to[0:PART, :] = (own[k * PART : (k + 1) * PART, :] + got[0:PART, :].astype(F32)).astype(BF)
    to[PART:, :] = pair_share(share, got_first)


def to_z1_body(own, got, share, got_first, got_own, to, kept, kept_share):
    to_z_body(1, own, got, share, got_first, to)
    kept[...] = own[0:PART, :] + got_own[...].astype(F32)
    kept_share[...] = pair_share(share, got_first)


def after_z_body(kept, share, r1, r2, r3, to_v):
    total = kept[...] + r1[0:PART, :].astype(F32)
    to_v[0:PART, :] = total + (r2[0:PART, :].astype(F32) + r3[0:PART, :].astype(F32))
    pair = share[...].astype(F32) + r1[PART:, :].astype(F32)
    to_v[PART:, :] = pair + (r2[PART:, :].astype(F32) + r3[PART:, :].astype(F32))


def after_v_body(mine, got, piece, share):
    piece[...] = (mine[0:PART, :] + got[0:PART, :]).astype(BF)
    put_split(share, 0, mine[PART:, :] + got[PART:, :])


def finish_body(p0, p3, p2, p1, grad_features):
    me = place()
    for k, piece in enumerate((p0, p1, p2, p3)):
        grad_features[at(chunk_of(me, me["x"] ^ k), PART), :] = piece[...]


def finish_weight_body(w0, w3, w2, w1, grad_weight):
    me = place()
    for k, share in enumerate((w0, w1, w2, w3)):
        grad_weight[at(me["x"] ^ k, SLICE), :] = get_split(share, 0)


def on_device(features, weight, cotangent, tile_values, tile_slots, tile_count):
    part = ((PART, WIDTH), BF)
    part32 = ((PART, WIDTH), F32)
    block = ((BLOCK, WIDTH), BF)
    block32 = ((BLOCK, WIDTH), F32)
    share32 = ((SLICE, WIDTH), F32)
    share16 = ((SLICE, WIDTH), BF)
    two = ((2 * PART, WIDTH), BF)
    to_z = ((PART + SLICE, WIDTH), BF)
    dense_shape = ((4, BLOCK, BLOCK), BF)

    (chunk,) = call(chunk_body, [part], features, specs=[HBM], scratch=[pltpu.SemaphoreType.DMA])
    chunk = send(chunk, TO_COLUMN)
    dense, dense_t = call(
        dense_body, [dense_shape, dense_shape], tile_slots, tile_count, tile_values, specs=[SMEM, SMEM, VMEM]
    )
    chunk, dense, dense_t = lax.optimization_barrier((chunk, dense, dense_t))
    chunks = spread(chunk, FLIP_Z)
    c0, c3, c2, c1 = chunks
    mine = [call(pair_body, [two], c3, c0)[0], call(pair_body, [two], c2, c1)[0]]
    by_u = [send(value, FLIP_U) for value in mine]
    by_c = [send(value, FLIP_C) for value in mine]
    by_uc = [send(value, FLIP_C) for value in by_u]
    total = pltpu.VMEM((BLOCK, WIDTH), F32)
    (most,) = call(
        forward_body, [block32], dense, *mine[::-1], *by_c[::-1], *by_u[::-1], scratch=[pltpu.VMEM((3, BLOCK, WIDTH), BF)]
    )
    to3, to2, to1, own = call(
        forward_last_body, [part32] * 4, dense, *by_uc[::-1], most, scratch=[pltpu.VMEM((1, BLOCK, WIDTH), BF), total]
    )
    got = [send(value, route) for value, route in zip((to3, to2, to1), FLIP_X[::-1])]
    (mine,) = call(sum_body, [((2 * PART + SLICE, WIDTH), BF)], own, *got, cotangent)
    got = send(mine, FLIP_H)
    (message,) = call(layer_body, [two], mine, got, weight)
    (output,) = call(output_body, [((SLICE, WIDTH), BF)], message, weight)
    got = spread(message, FLIP_X)

    whole = pltpu.VMEM((BLOCK, WIDTH), BF)
    to_c, grad_agg = call(
        backward_body, [((BLOCK + SLICE, WIDTH), F32), block], dense_t, weight, *got,
        scratch=[whole, whole, pltpu.VMEM((WIDTH, WIDTH), F32)],
    )
    got = send(to_c, FLIP_C)
    (keep_u,) = call(keep_body, [block32], dense_t, grad_agg)
    *to_u, share = call(to_u_body, [to_z, part, part, part, share16], keep_u, to_c, got)
    u3, u2, u1, u0 = [send(value, FLIP_U) for value in to_u]
    to_c, keep = call(kept_body, [block32, block32], dense_t, grad_agg)
    (own,) = call(after_c_body, [block32], keep, send(to_c, FLIP_C), scratch=[total])
    (to3,) = call(functools.partial(to_z_body, 3), [to_z], own, u3, share, u3)
    (to2,) = call(functools.partial(to_z_body, 2), [to_z], own, u2, share, u3)
    to1, kept, share = call(to_z1_body, [to_z, part32, share16], own, u1, share, u3, u0)
    from_z = [send(value, route) for value, route in zip((to1, to2, to3), FLIP_Z)]
    (to_v,) = call(after_z_body, [((PART + SLICE, WIDTH), F32)], kept, share, *from_z)
    piece, share = call(after_v_body, [part, part], to_v, send(to_v, FLIP_V))
    piece = send(piece, TO_ROW)
    shares = spread(share, FLIP_X)
    pieces = spread(piece, FLIP_X)
    (grad_weight,) = call(finish_weight_body, [((WIDTH, WIDTH), F32)], *shares)
    (grad_features,) = call(finish_body, [block], *pieces)
    return output, grad_weight, grad_features


def solution(mesh):
    placed = (
        P("rows", None),
        P(),
        P(("rows", "rep"), None),
        P("rows", "rep", None, None, None),
        P("rows", "rep", None),
        P("rows", "rep"),
    )
    return jax.shard_map(
        on_device,
        mesh=mesh,
        in_specs=placed,
        out_specs=(P(("rows", "rep"), None), P(), P("rows", None)),
        check_vma=False,
    )
```

```python
import functools
import itertools

import jax
import jax.numpy as jnp
from jax import lax
from jax.experimental import pallas as pl
from jax.experimental.pallas import tpu as pltpu
from jax.sharding import PartitionSpec as P

BF = jnp.bfloat16
F32 = jnp.float32
TILE = 128
WIDTH = 256
BLOCK = 512
PART = 128
SLICE = 64
AXES = ("rows", "rep")


def u_of(y):
    return (y ^ (y >> 1)) & 1


def v_of(y):
    return y >> 1


Y_OF = {(u_of(y), v_of(y)): y for y in range(4)}
PLACES = list(itertools.product(range(4), range(4), range(2), range(4), range(2)))


def index_of(z, y, c, x, h):
    return (z * 8 + y * 2 + c) * 8 + x * 2 + h


def pairs(target):
    return [(index_of(*place), index_of(*target(*place))) for place in PLACES]


FLIP_C = pairs(lambda z, y, c, x, h: (z, y, 1 - c, x, h))
FLIP_U = pairs(lambda z, y, c, x, h: (z, Y_OF[1 - u_of(y), v_of(y)], c, x, h))
FLIP_V = pairs(lambda z, y, c, x, h: (z, Y_OF[u_of(y), 1 - v_of(y)], c, x, h))
FLIP_H = pairs(lambda z, y, c, x, h: (z, y, c, x, 1 - h))
FLIP_X = [pairs(lambda z, y, c, x, h, k=k: (z, y, c, x ^ k, h)) for k in (1, 2, 3)]
FLIP_Z = [pairs(lambda z, y, c, x, h, k=k: (z ^ k, y, c, x, h)) for k in (1, 2, 3)]
ROUTE = (((2, 1, 3, 0), (0, 3, 2, 1), (2, 1, 0, 3), (3, 0, 2, 1)), ((0, 1, 3, 2), (0, 1, 2, 3), (0, 1, 2, 3), (1, 0, 2, 3)))
TO_ROW = pairs(lambda z, y, c, x, h: (x, Y_OF[u_of(y), h], c, ROUTE[v_of(y) == h][x][z], 1 - v_of(y)))
TO_COLUMN = [(there, here) for here, there in TO_ROW]
TO_ROW_TOO = pairs(lambda z, y, c, x, h: (x, Y_OF[u_of(y), h], c, ROUTE[1 - v_of(y) == h][x][z], v_of(y)))


def chunk_table(same):
    word = sum((z << (8 * x + 2 * ROUTE[same][x][z])) for x in range(4) for z in range(4))
    return word - (1 << 32) if word >> 31 else word


CHUNKS = (chunk_table(0), chunk_table(1))


def send(value, route):
    return lax.ppermute(value, AXES, route)


def spread(value, routes):
    return [value] + [send(value, route) for route in routes[::-1]]


def place():
    r = lax.axis_index("rows")
    p = lax.axis_index("rep")
    y = (r >> 1) & 3
    v = y >> 1
    return dict(z=r >> 3, c=r & 1, u=(y ^ v) & 1, v=v, x=p >> 1, h=p & 1)


def chunk_of(me, x):
    word = jnp.where((1 - me["h"]) == me["v"], jnp.int32(CHUNKS[1]), jnp.int32(CHUNKS[0]))
    return (word >> (8 * me["z"] + 2 * x)) & 3


def at(index, size):
    return pl.ds(pl.multiple_of(index * size, size), size)


def dot(a, b, dims=((1,), (0,))):
    return lax.dot_general(a, b, (dims, ((), ())), preferred_element_type=F32)


SMEM = pl.BlockSpec(memory_space=pltpu.SMEM)
VMEM = pl.BlockSpec(memory_space=pltpu.VMEM)
HBM = pl.BlockSpec(memory_space=pl.ANY)


def call(body, outs, *args, specs=None, scratch=()):
    return pl.pallas_call(
        body,
        out_shape=[jax.ShapeDtypeStruct(shape, dtype) for shape, dtype in outs],
        in_specs=specs or [VMEM] * len(args),
        out_specs=[VMEM] * len(outs),
        scratch_shapes=list(scratch),
        compiler_params=pltpu.CompilerParams(vmem_limit_bytes=24 * 2**20),
    )(*args)


def split(value):
    high = value.astype(BF)
    return high, (value - high.astype(F32)).astype(BF)


def put_split(ref, start, value):
    high, low = split(value)
    ref[start : start + SLICE, :] = high
    ref[start + SLICE : start + 2 * SLICE, :] = low


def get_split(ref, start):
    return ref[start : start + SLICE, :].astype(F32) + ref[start + SLICE : start + 2 * SLICE, :].astype(F32)


def chunk_body(features, out, sem):
    me = place()
    copy = pltpu.make_async_copy(features.at[at(chunk_of(me, me["x"]), PART), :], out, sem)
    copy.start()
    copy.wait()


def dense_body(slots, count, tiles, dense, dense_t):
    me = place()
    dense[...] = jnp.zeros_like(dense)
    dense_t[...] = jnp.zeros_like(dense_t)
    for k in range(4):
        b = ((me["u"] ^ me["h"]) * 2 + me["c"]) ^ k
        for s in range(2):
            slot = slots[0, b, s]
            tile = jnp.where(s < count[0, b], tiles[0, b, s], jnp.zeros((), BF))

            @pl.when(s < count[0, b])
            def _():
                dense[k, at(slot >> 2, TILE), at(slot & 3, TILE)] = tile
                dense_t[k, at(slot & 3, TILE), at(slot >> 2, TILE)] = tile.T


def pair_body(low, high, out):
    out[0:PART, :] = low[...]
    out[PART:, :] = high[...]


def put_block(me, blocks, i, first, second):
    for k, part in ((3, first[0:PART, :]), (0, first[PART:, :]), (2, second[0:PART, :]), (1, second[PART:, :])):
        blocks[i, at(me["z"] ^ k, PART), :] = part


def forward_body(dense, b0, a0, b1, a1, b2, a2, total, blocks):
    me = place()
    for i, (first, second) in enumerate(((a0, b0), (a1, b1), (a2, b2))):
        put_block(me, blocks, i, first, second)
    total[...] = dot(dense[0], blocks[0]) + dot(dense[1], blocks[1]) + dot(dense[2], blocks[2])


def forward_last_body(dense, b3, a3, most, to3, to2, to1, own, blocks, total):
    me = place()
    put_block(me, blocks, 0, a3, b3)
    total[...] = most[...] + dot(dense[3], blocks[0])
    for k, to in enumerate((own, to1, to2, to3)):
        to[...] = total[at(me["x"] ^ k, PART), :]


def sum_body(own, r3, r2, r1, cot, to_h):
    total = own[...] + r1[...] + (r2[...] + r3[...])
    high, low = split(total)
    to_h[0:PART, :] = high
    to_h[PART : 2 * PART, :] = low
    to_h[2 * PART :, :] = cot[...]


def aggregate_of(mine, got):
    parts = [ref[0:PART, :].astype(F32) + ref[PART : 2 * PART, :].astype(F32) for ref in (mine, got)]
    return (parts[0] + parts[1]).astype(BF)


def layer_body(mine, got, weight, message):
    aggregate = aggregate_of(mine, got)
    preact = dot(aggregate, weight[...])
    gates = jax.nn.sigmoid(preact)
    first = place()["h"] == 0
    a, b = mine[2 * PART :, :], got[2 * PART :, :]
    cotangent = jnp.concatenate([jnp.where(first, a, b), jnp.where(first, b, a)], axis=0).astype(F32)
    message[0:PART, :] = aggregate
    message[PART:, :] = (cotangent * gates * (1.0 + preact * (1.0 - gates))).astype(BF)


def output_body(message, weight, output):
    own = message[at(place()["h"], SLICE), :]
    preact = dot(own, weight[...])
    output[...] = (preact * jax.nn.sigmoid(preact)).astype(BF)


def backward_body(dense_t, weight, m0, m3, m2, m1, to_c, grad_agg, aggregate, grad_pre, grad_w):
    me = place()
    for k, m in enumerate((m0, m1, m2, m3)):
        rows = at(me["x"] ^ k, PART)
        aggregate[rows, :] = m[0:PART, :]
        grad_pre[rows, :] = m[PART:, :]
    grad = dot(grad_pre[...], weight[...], ((1,), (1,))).astype(BF)
    grad_agg[...] = grad
    to_c[0:BLOCK, :] = dot(dense_t[3], grad)
    grad_w[...] = dot(aggregate[...], grad_pre[...], ((0,), (0,)))
    to_c[BLOCK:, :] = grad_w[at(me["x"], SLICE), :]


def keep_body(dense_t, grad_agg, keep):
    keep[...] = dot(dense_t[2], grad_agg[...])


def to_u_body(keep, mine, got, u3, u2, u1, u0, share):
    me = place()
    for k, out in ((3, u3), (2, u2), (1, u1), (0, u0)):
        rows = at(me["z"] ^ k, PART)
        out[0:PART, :] = (keep[rows, :] + got[rows, :]).astype(BF)
    both = (mine[BLOCK:, :] + got[BLOCK:, :]).astype(BF)
    u3[PART:, :] = both
    share[...] = both


def kept_body(dense_t, grad_agg, to_c, keep):
    to_c[...] = dot(dense_t[1], grad_agg[...])
    keep[...] = dot(dense_t[0], grad_agg[...])


def after_c_body(keep, got, own, total):
    me = place()
    total[...] = keep[...] + got[...]
    for k in range(4):
        own[k * PART : (k + 1) * PART, :] = total[at(me["z"] ^ k, PART), :]


def pair_share(share, got_first):
    return (share[...].astype(F32) + got_first[PART:, :].astype(F32)).astype(BF)


def to_z_body(k, own, got, share, got_first, to):
    to[0:PART, :] = (own[k * PART : (k + 1) * PART, :] + got[0:PART, :].astype(F32)).astype(BF)
    to[PART:, :] = pair_share(share, got_first)


def to_z1_body(own, got, share, got_first, got_own, to, kept, kept_share):
    to_z_body(1, own, got, share, got_first, to)
    kept[...] = own[0:PART, :] + got_own[...].astype(F32)
    kept_share[...] = pair_share(share, got_first)


def after_z_body(kept, share, r1, r2, r3, piece, total_share):
    total = kept[...] + r1[0:PART, :].astype(F32)
    piece[...] = (total + (r2[0:PART, :].astype(F32) + r3[0:PART, :].astype(F32))).astype(BF)
    pair = share[...].astype(F32) + r1[PART:, :].astype(F32)
    total_share[...] = pair + (r2[PART:, :].astype(F32) + r3[PART:, :].astype(F32))


def last_body(one, two, mine, got, message):
    message[0:PART, :] = (one[...].astype(F32) + two[...].astype(F32)).astype(BF)
    put_split(message, PART, mine[...] + got[...])


def finish_body(m0, m3, m2, m1, grad_features, grad_weight):
    me = place()
    for k, message in enumerate((m0, m1, m2, m3)):
        grad_features[at(chunk_of(me, me["x"] ^ k), PART), :] = message[0:PART, :]
        grad_weight[at(me["x"] ^ k, SLICE), :] = get_split(message, PART)


def on_device(features, weight, cotangent, tile_values, tile_slots, tile_count):
    part = ((PART, WIDTH), BF)
    part32 = ((PART, WIDTH), F32)
    block = ((BLOCK, WIDTH), BF)
    block32 = ((BLOCK, WIDTH), F32)
    share32 = ((SLICE, WIDTH), F32)
    share16 = ((SLICE, WIDTH), BF)
    two = ((2 * PART, WIDTH), BF)
    to_z = ((PART + SLICE, WIDTH), BF)
    dense_shape = ((4, BLOCK, BLOCK), BF)

    (chunk,) = call(chunk_body, [part], features, specs=[HBM], scratch=[pltpu.SemaphoreType.DMA])
    chunk = send(chunk, TO_COLUMN)
    dense, dense_t = call(
        dense_body, [dense_shape, dense_shape], tile_slots, tile_count, tile_values, specs=[SMEM, SMEM, VMEM]
    )
    chunk, dense, dense_t = lax.optimization_barrier((chunk, dense, dense_t))
    chunks = spread(chunk, FLIP_Z)
    c0, c3, c2, c1 = chunks
    mine = [call(pair_body, [two], c3, c0)[0], call(pair_body, [two], c2, c1)[0]]
    by_u = [send(value, FLIP_U) for value in mine]
    by_c = [send(value, FLIP_C) for value in mine]
    by_uc = [send(value, FLIP_C) for value in by_u]
    total = pltpu.VMEM((BLOCK, WIDTH), F32)
    (most,) = call(
        forward_body, [block32], dense, *mine[::-1], *by_c[::-1], *by_u[::-1], scratch=[pltpu.VMEM((3, BLOCK, WIDTH), BF)]
    )
    to3, to2, to1, own = call(
        forward_last_body, [part32] * 4, dense, *by_uc[::-1], most, scratch=[pltpu.VMEM((1, BLOCK, WIDTH), BF), total]
    )
    got = [send(value, route) for value, route in zip((to3, to2, to1), FLIP_X[::-1])]
    (mine,) = call(sum_body, [((2 * PART + SLICE, WIDTH), BF)], own, *got, cotangent)
    got = send(mine, FLIP_H)
    (message,) = call(layer_body, [two], mine, got, weight)
    (output,) = call(output_body, [((SLICE, WIDTH), BF)], message, weight)
    got = spread(message, FLIP_X)

    whole = pltpu.VMEM((BLOCK, WIDTH), BF)
    to_c, grad_agg = call(
        backward_body, [((BLOCK + SLICE, WIDTH), F32), block], dense_t, weight, *got,
        scratch=[whole, whole, pltpu.VMEM((WIDTH, WIDTH), F32)],
    )
    got = send(to_c, FLIP_C)
    (keep_u,) = call(keep_body, [block32], dense_t, grad_agg)
    *to_u, share = call(to_u_body, [to_z, part, part, part, share16], keep_u, to_c, got)
    u3, u2, u1, u0 = [send(value, FLIP_U) for value in to_u]
    to_c, keep = call(kept_body, [block32, block32], dense_t, grad_agg)
    (own,) = call(after_c_body, [block32], keep, send(to_c, FLIP_C), scratch=[total])
    (to3,) = call(functools.partial(to_z_body, 3), [to_z], own, u3, share, u3)
    (to2,) = call(functools.partial(to_z_body, 2), [to_z], own, u2, share, u3)
    to1, kept, share = call(to_z1_body, [to_z, part32, share16], own, u1, share, u3, u0)
    from_z = [send(value, route) for value, route in zip((to1, to2, to3), FLIP_Z)]
    piece, share = call(after_z_body, [part, share32], kept, share, *from_z)
    routes = (TO_ROW, TO_ROW_TOO)
    (message,) = call(last_body, [two], *[send(piece, route) for route in routes], share, send(share, FLIP_V))
    grad_features, grad_weight = call(finish_body, [block, ((WIDTH, WIDTH), F32)], *spread(message, FLIP_X))
    return output, grad_weight, grad_features


def solution(mesh):
    placed = (
        P("rows", None),
        P(),
        P(("rows", "rep"), None),
        P("rows", "rep", None, None, None),
        P("rows", "rep", None),
        P("rows", "rep"),
    )
    return jax.shard_map(
        on_device,
        mesh=mesh,
        in_specs=placed,
        out_specs=(P(("rows", "rep"), None), P(), P("rows", None)),
        check_vma=False,
    )
```

```python
import itertools

import jax
import jax.numpy as jnp
from jax import lax
from jax.experimental import pallas as pl
from jax.experimental.pallas import tpu as pltpu
from jax.sharding import PartitionSpec as P

BF = jnp.bfloat16
F32 = jnp.float32
TILE = 128
WIDTH = 256
BLOCK = 512
PART = 128
SLICE = 64
AXES = ("rows", "rep")


def u_of(y):
    return (y ^ (y >> 1)) & 1


def v_of(y):
    return y >> 1


Y_OF = {(u_of(y), v_of(y)): y for y in range(4)}
PLACES = list(itertools.product(range(4), range(4), range(2), range(4), range(2)))


def index_of(z, y, c, x, h):
    return (z * 8 + y * 2 + c) * 8 + x * 2 + h


def pairs(target):
    return [(index_of(*place), index_of(*target(*place))) for place in PLACES]


FLIP_C = pairs(lambda z, y, c, x, h: (z, y, 1 - c, x, h))
FLIP_U = pairs(lambda z, y, c, x, h: (z, Y_OF[1 - u_of(y), v_of(y)], c, x, h))
FLIP_V = pairs(lambda z, y, c, x, h: (z, Y_OF[u_of(y), 1 - v_of(y)], c, x, h))
FLIP_H = pairs(lambda z, y, c, x, h: (z, y, c, x, 1 - h))
FLIP_X = [pairs(lambda z, y, c, x, h, k=k: (z, y, c, x ^ k, h)) for k in (1, 2, 3)]
FLIP_Z = [pairs(lambda z, y, c, x, h, k=k: (z ^ k, y, c, x, h)) for k in (1, 2, 3)]
ROUTE = (((2, 1, 3, 0), (0, 3, 2, 1), (2, 1, 0, 3), (3, 0, 2, 1)), ((0, 1, 3, 2), (0, 1, 2, 3), (0, 1, 2, 3), (1, 0, 2, 3)))
TO_ROW = pairs(lambda z, y, c, x, h: (x, Y_OF[u_of(y), h], c, ROUTE[v_of(y) == h][x][z], 1 - v_of(y)))
TO_COLUMN = [(there, here) for here, there in TO_ROW]


def chunk_table(same):
    word = sum((z << (8 * x + 2 * ROUTE[same][x][z])) for x in range(4) for z in range(4))
    return word - (1 << 32) if word >> 31 else word


CHUNKS = (chunk_table(0), chunk_table(1))


def send(value, route):
    return lax.ppermute(value, AXES, route)


def spread(value, routes):
    return [value] + [send(value, route) for route in routes[::-1]]


def place():
    r = lax.axis_index("rows")
    p = lax.axis_index("rep")
    y = (r >> 1) & 3
    v = y >> 1
    return dict(z=r >> 3, c=r & 1, u=(y ^ v) & 1, v=v, x=p >> 1, h=p & 1)


def chunk_of(me, x):
    word = jnp.where((1 - me["h"]) == me["v"], jnp.int32(CHUNKS[1]), jnp.int32(CHUNKS[0]))
    return (word >> (8 * me["z"] + 2 * x)) & 3


def at(index, size):
    return pl.ds(pl.multiple_of(index * size, size), size)


def dot(a, b, dims=((1,), (0,))):
    return lax.dot_general(a, b, (dims, ((), ())), preferred_element_type=F32)


SMEM = pl.BlockSpec(memory_space=pltpu.SMEM)
VMEM = pl.BlockSpec(memory_space=pltpu.VMEM)
HBM = pl.BlockSpec(memory_space=pl.ANY)


def call(body, outs, *args, specs=None, scratch=()):
    return pl.pallas_call(
        body,
        out_shape=[jax.ShapeDtypeStruct(shape, dtype) for shape, dtype in outs],
        in_specs=specs or [VMEM] * len(args),
        out_specs=[VMEM] * len(outs),
        scratch_shapes=list(scratch),
        compiler_params=pltpu.CompilerParams(vmem_limit_bytes=24 * 2**20),
    )(*args)


def split(value):
    high = value.astype(BF)
    return high, (value - high.astype(F32)).astype(BF)


def put_split(ref, start, value):
    high, low = split(value)
    ref[start : start + SLICE, :] = high
    ref[start + SLICE : start + 2 * SLICE, :] = low


def get_split(ref, start):
    return ref[start : start + SLICE, :].astype(F32) + ref[start + SLICE : start + 2 * SLICE, :].astype(F32)


def chunk_body(features, out, sem):
    me = place()
    copy = pltpu.make_async_copy(features.at[at(chunk_of(me, me["x"]), PART), :], out, sem)
    copy.start()
    copy.wait()


def dense_body(slots, count, tiles, dense, dense_t):
    me = place()
    dense[...] = jnp.zeros_like(dense)
    dense_t[...] = jnp.zeros_like(dense_t)
    for k in range(4):
        b = ((me["u"] ^ me["h"]) * 2 + me["c"]) ^ k
        for s in range(2):
            slot = slots[0, b, s]
            tile = jnp.where(s < count[0, b], tiles[0, b, s], jnp.zeros((), BF))

            @pl.when(s < count[0, b])
            def _():
                dense[k, at(slot >> 2, TILE), at(slot & 3, TILE)] = tile
                dense_t[k, at(slot & 3, TILE), at(slot >> 2, TILE)] = tile.T


def pair_body(low, high, out):
    out[0:PART, :] = low[...]
    out[PART:, :] = high[...]


def put_block(me, blocks, i, first, second):
    for k, part in ((3, first[0:PART, :]), (0, first[PART:, :]), (2, second[0:PART, :]), (1, second[PART:, :])):
        blocks[i, at(me["z"] ^ k, PART), :] = part


def forward_body(dense, b0, a0, b1, a1, b2, a2, total, blocks):
    me = place()
    for i, (first, second) in enumerate(((a0, b0), (a1, b1), (a2, b2))):
        put_block(me, blocks, i, first, second)
    total[...] = dot(dense[0], blocks[0]) + dot(dense[1], blocks[1]) + dot(dense[2], blocks[2])


def forward_last_body(dense, b3, a3, most, to3, to2, to1, own, blocks, total):
    me = place()
    put_block(me, blocks, 0, a3, b3)
    total[...] = most[...] + dot(dense[3], blocks[0])
    for k, to in enumerate((own, to1, to2, to3)):
        to[...] = total[at(me["x"] ^ k, PART), :].astype(to.dtype)


def sum_body(own, r3, r2, r1, cot, to_h):
    total = own[...] + r1[...] + (r2[...].astype(F32) + r3[...])
    high, low = split(total)
    to_h[0:PART, :] = high
    to_h[PART : 2 * PART, :] = low
    to_h[2 * PART :, :] = cot[...]


def aggregate_of(mine, got):
    parts = [ref[0:PART, :].astype(F32) + ref[PART : 2 * PART, :].astype(F32) for ref in (mine, got)]
    return (parts[0] + parts[1]).astype(BF)


def layer_body(mine, got, weight, to3, to2, to1, own, aggregate, share, grad_w):
    me = place()
    agg = aggregate_of(mine, got)
    preact = dot(agg, weight[...])
    gates = jax.nn.sigmoid(preact)
    first = me["h"] == 0
    a, b = mine[2 * PART :, :], got[2 * PART :, :]
    cotangent = jnp.concatenate([jnp.where(first, a, b), jnp.where(first, b, a)], axis=0).astype(F32)
    grad_pre = (cotangent * gates * (1.0 + preact * (1.0 - gates))).astype(BF)
    grad_w[...] = dot(agg, grad_pre, ((0,), (0,)))
    aggregate[...] = agg
    own[...] = grad_pre
    share[...] = grad_w[at(me["x"], SLICE), :]
    for k, to in ((3, to3), (2, to2), (1, to1)):
        to[0:PART, :] = grad_pre
        to[PART:, :] = grad_w[at(me["x"] ^ k, SLICE), :].astype(BF)


def output_body(aggregate, weight, output):
    preact = dot(aggregate[at(place()["h"], SLICE), :], weight[...])
    output[...] = (preact * jax.nn.sigmoid(preact)).astype(BF)


def backward_body(dense_t, weight, m0, m3, m2, m1, share, to_c, grad_agg, grad_pre):
    me = place()
    for k, m in enumerate((m0, m1, m2, m3)):
        grad_pre[at(me["x"] ^ k, PART), :] = m[0:PART, :]
    grad = dot(grad_pre[...], weight[...], ((1,), (1,))).astype(BF)
    grad_agg[...] = grad
    to_c[0:BLOCK, :] = dot(dense_t[3], grad)
    total = share[...] + m1[PART:, :].astype(F32)
    to_c[BLOCK:, :] = total + (m2[PART:, :].astype(F32) + m3[PART:, :].astype(F32))


def keep_body(dense_t, grad_agg, keep):
    keep[...] = dot(dense_t[2], grad_agg[...])


def to_u_body(keep, mine, got, u3, u2, u1, u0, share):
    me = place()
    for k, out in ((3, u3), (2, u2), (1, u1), (0, u0)):
        rows = at(me["z"] ^ k, PART)
        out[0:PART, :] = (keep[rows, :] + got[rows, :]).astype(BF)
    both = (mine[BLOCK:, :] + got[BLOCK:, :]).astype(BF)
    u3[PART:, :] = both
    share[...] = both


def kept_body(dense_t, grad_agg, to_c, keep):
    to_c[...] = dot(dense_t[1], grad_agg[...])
    keep[...] = dot(dense_t[0], grad_agg[...])


def after_c_body(keep, got, own, total):
    me = place()
    total[...] = keep[...] + got[...]
    for k in range(4):
        own[k * PART : (k + 1) * PART, :] = total[at(me["z"] ^ k, PART), :]


def to_z_body(k, own, got, to):
    to[...] = (own[k * PART : (k + 1) * PART, :] + got[0:PART, :].astype(F32)).astype(BF)


def to_z3_body(own, got, to):
    to_z_body(3, own, got, to)


def to_z2_body(own, got, earlier, to):
    to_z_body(2, own, got, to)


def to_z1_body(own, got, got_own, share, earlier, to, kept, total):
    to_z_body(1, own, got, to)
    kept[...] = own[0:PART, :] + got_own[...].astype(F32)
    total[...] = share[...].astype(F32) + earlier[PART:, :].astype(F32)


def after_z_body(kept, r1, r2, r3, mine, got, to_v, share):
    total = kept[...] + r1[...].astype(F32)
    to_v[...] = total + (r2[...].astype(F32) + r3[...].astype(F32))
    share[...] = mine[...] + got[...]


def after_v_body(one, two, mine, got, piece, share):
    piece[...] = (one[...] + two[...]).astype(BF)
    share[...] = mine[...] + got[...]


def last_body(piece, mine, got, message):
    message[0:PART, :] = piece[...]
    put_split(message, PART, mine[...] + got[...])


def finish_body(m0, m3, m2, m1, grad_features, grad_weight):
    me = place()
    for k, message in enumerate((m0, m1, m2, m3)):
        grad_features[at(chunk_of(me, me["x"] ^ k), PART), :] = message[0:PART, :]
        grad_weight[at(me["x"] ^ k, SLICE), :] = get_split(message, PART)


def on_device(features, weight, cotangent, tile_values, tile_slots, tile_count):
    part = ((PART, WIDTH), BF)
    part32 = ((PART, WIDTH), F32)
    block = ((BLOCK, WIDTH), BF)
    block32 = ((BLOCK, WIDTH), F32)
    share32 = ((SLICE, WIDTH), F32)
    share16 = ((SLICE, WIDTH), BF)
    two = ((2 * PART, WIDTH), BF)
    to_z = ((PART + SLICE, WIDTH), BF)
    dense_shape = ((4, BLOCK, BLOCK), BF)

    (chunk,) = call(chunk_body, [part], features, specs=[HBM], scratch=[pltpu.SemaphoreType.DMA])
    chunk = send(chunk, TO_COLUMN)
    dense, dense_t = call(
        dense_body, [dense_shape, dense_shape], tile_slots, tile_count, tile_values, specs=[SMEM, SMEM, VMEM]
    )
    chunk, dense, dense_t = lax.optimization_barrier((chunk, dense, dense_t))
    chunks = spread(chunk, FLIP_Z)
    c0, c3, c2, c1 = chunks
    mine = [call(pair_body, [two], c3, c0)[0], call(pair_body, [two], c2, c1)[0]]
    by_u = [send(value, FLIP_U) for value in mine]
    by_c = [send(value, FLIP_C) for value in mine]
    by_uc = [send(value, FLIP_C) for value in by_u]
    total = pltpu.VMEM((BLOCK, WIDTH), F32)
    (most,) = call(
        forward_body, [block32], dense, *mine[::-1], *by_c[::-1], *by_u[::-1], scratch=[pltpu.VMEM((3, BLOCK, WIDTH), BF)]
    )
    to3, to2, to1, own = call(
        forward_last_body, [part32, part, part32, part32], dense, *by_uc[::-1], most, scratch=[pltpu.VMEM((1, BLOCK, WIDTH), BF), total]
    )
    got = [send(value, route) for value, route in zip((to3, to2, to1), FLIP_X[::-1])]
    (mine,) = call(sum_body, [((2 * PART + SLICE, WIDTH), BF)], own, *got, cotangent)
    got = send(mine, FLIP_H)
    *to, own, aggregate, share = call(
        layer_body, [to_z, to_z, to_z, part, part, share32], mine, got, weight, scratch=[pltpu.VMEM((WIDTH, WIDTH), F32)]
    )
    (output,) = call(output_body, [((SLICE, WIDTH), BF)], aggregate, weight)
    got = [send(value, route) for value, route in zip(to, FLIP_X[::-1])]
    to_c, grad_agg = call(
        backward_body, [((BLOCK + SLICE, WIDTH), F32), block], dense_t, weight, own, *got, share,
        scratch=[pltpu.VMEM((BLOCK, WIDTH), BF)],
    )
    got = send(to_c, FLIP_C)
    (keep_u,) = call(keep_body, [block32], dense_t, grad_agg)
    *to_u, share = call(to_u_body, [to_z, part, part, part, share16], keep_u, to_c, got)
    u3, u2, u1, u0 = [send(value, FLIP_U) for value in to_u]
    to_c, keep = call(kept_body, [block32, block32], dense_t, grad_agg)
    (own,) = call(after_c_body, [block32], keep, send(to_c, FLIP_C), scratch=[total])
    (to3,) = call(to_z3_body, [part], own, u3)
    (to2,) = call(to_z2_body, [part], own, u2, u3)
    to1, kept, share = call(to_z1_body, [part, part32, share32], own, u1, u0, share, u3)
    from_z = [send(value, route) for value, route in zip((to1, to2, to3), FLIP_Z)]
    to_v, share = call(after_z_body, [part32, share32], kept, *from_z, share, send(share, FLIP_Z[0]))
    piece, share = call(
        after_v_body, [part, share32], to_v, send(to_v, FLIP_V), share, send(share, FLIP_Z[1])
    )
    (message,) = call(last_body, [two], send(piece, TO_ROW), share, send(share, FLIP_V))
    grad_features, grad_weight = call(finish_body, [block, ((WIDTH, WIDTH), F32)], *spread(message, FLIP_X))
    return output, grad_weight, grad_features


def solution(mesh):
    placed = (
        P("rows", None),
        P(),
        P(("rows", "rep"), None),
        P("rows", "rep", None, None, None),
        P("rows", "rep", None),
        P("rows", "rep"),
    )
    return jax.shard_map(
        on_device,
        mesh=mesh,
        in_specs=placed,
        out_specs=(P(("rows", "rep"), None), P(), P("rows", None)),
        check_vma=False,
    )
```

```python
import itertools

import jax
import jax.numpy as jnp
from jax import lax
from jax.experimental import pallas as pl
from jax.experimental.pallas import tpu as pltpu
from jax.sharding import PartitionSpec as P

BF = jnp.bfloat16
F32 = jnp.float32
TILE = 128
WIDTH = 256
BLOCK = 512
PART = 128
SLICE = 64
AXES = ("rows", "rep")


def u_of(y):
    return (y ^ (y >> 1)) & 1


def v_of(y):
    return y >> 1


Y_OF = {(u_of(y), v_of(y)): y for y in range(4)}
PLACES = list(itertools.product(range(4), range(4), range(2), range(4), range(2)))


def index_of(z, y, c, x, h):
    return (z * 8 + y * 2 + c) * 8 + x * 2 + h


def pairs(target):
    return [(index_of(*place), index_of(*target(*place))) for place in PLACES]


FLIP_C = pairs(lambda z, y, c, x, h: (z, y, 1 - c, x, h))
FLIP_U = pairs(lambda z, y, c, x, h: (z, Y_OF[1 - u_of(y), v_of(y)], c, x, h))
FLIP_V = pairs(lambda z, y, c, x, h: (z, Y_OF[u_of(y), 1 - v_of(y)], c, x, h))
FLIP_H = pairs(lambda z, y, c, x, h: (z, y, c, x, 1 - h))
FLIP_X = [pairs(lambda z, y, c, x, h, k=k: (z, y, c, x ^ k, h)) for k in (1, 2, 3)]
FLIP_Z = [pairs(lambda z, y, c, x, h, k=k: (z ^ k, y, c, x, h)) for k in (1, 2, 3)]
FAR_X = (FLIP_X[1], FLIP_X[2], FLIP_X[0])
ROUTE = (((2, 1, 3, 0), (0, 3, 2, 1), (2, 1, 0, 3), (3, 0, 2, 1)), ((0, 1, 3, 2), (0, 1, 2, 3), (0, 1, 2, 3), (1, 0, 2, 3)))
TO_ROW = pairs(lambda z, y, c, x, h: (x, Y_OF[u_of(y), h], c, ROUTE[v_of(y) == h][x][z], 1 - v_of(y)))
TO_COLUMN = [(there, here) for here, there in TO_ROW]


def chunk_table(same):
    word = sum((z << (8 * x + 2 * ROUTE[same][x][z])) for x in range(4) for z in range(4))
    return word - (1 << 32) if word >> 31 else word


CHUNKS = (chunk_table(0), chunk_table(1))


def send(value, route):
    return lax.ppermute(value, AXES, route)


def place():
    r = lax.axis_index("rows")
    p = lax.axis_index("rep")
    y = (r >> 1) & 3
    v = y >> 1
    return dict(z=r >> 3, c=r & 1, u=(y ^ v) & 1, v=v, x=p >> 1, h=p & 1)


def chunk_of(me, x):
    word = jnp.where((1 - me["h"]) == me["v"], jnp.int32(CHUNKS[1]), jnp.int32(CHUNKS[0]))
    return (word >> (8 * me["z"] + 2 * x)) & 3


def at(index, size):
    return pl.ds(pl.multiple_of(index * size, size), size)


def dot(a, b, dims=((1,), (0,))):
    return lax.dot_general(a, b, (dims, ((), ())), preferred_element_type=F32)


SMEM = pl.BlockSpec(memory_space=pltpu.SMEM)
VMEM = pl.BlockSpec(memory_space=pltpu.VMEM)
HBM = pl.BlockSpec(memory_space=pl.ANY)


def call(body, outs, *args, specs=None, scratch=()):
    return pl.pallas_call(
        body,
        out_shape=[jax.ShapeDtypeStruct(shape, dtype) for shape, dtype in outs],
        in_specs=specs or [VMEM] * len(args),
        out_specs=[VMEM] * len(outs),
        scratch_shapes=list(scratch),
        compiler_params=pltpu.CompilerParams(vmem_limit_bytes=24 * 2**20),
    )(*args)


def split(value):
    high = value.astype(BF)
    return high, (value - high.astype(F32)).astype(BF)


def put_split(ref, start, value):
    high, low = split(value)
    ref[start : start + SLICE, :] = high
    ref[start + SLICE : start + 2 * SLICE, :] = low


def get_split(ref, start):
    return ref[start : start + SLICE, :].astype(F32) + ref[start + SLICE : start + 2 * SLICE, :].astype(F32)


def half_body(features, out, sem):
    me = place()
    half = chunk_of(me, me["x"]) & 1
    copy = pltpu.make_async_copy(features.at[at(half, 2 * PART), :], out, sem)
    copy.start()
    copy.wait()


def dense_body(slots, count, tiles, dense, dense_t):
    me = place()
    dense[...] = jnp.zeros_like(dense)
    dense_t[...] = jnp.zeros_like(dense_t)
    for k in range(4):
        b = ((me["u"] ^ me["h"]) * 2 + me["c"]) ^ k
        for s in range(2):
            slot = slots[0, b, s]
            tile = jnp.where(s < count[0, b], tiles[0, b, s], jnp.zeros((), BF))

            @pl.when(s < count[0, b])
            def _():
                dense[k, at(slot >> 2, TILE), at(slot & 3, TILE)] = tile
                dense_t[k, at(slot & 3, TILE), at(slot >> 2, TILE)] = tile.T


def put_block(me, blocks, i, mine, other):
    half = me["z"] & 1
    blocks[i, at(half, 2 * PART), :] = mine[...]
    blocks[i, at(1 - half, 2 * PART), :] = other[...]


def forward_body(dense, b0, a0, b1, a1, b2, a2, total, blocks):
    me = place()
    for i, (first, second) in enumerate(((a0, b0), (a1, b1), (a2, b2))):
        put_block(me, blocks, i, first, second)
    total[...] = dot(dense[0], blocks[0]) + dot(dense[1], blocks[1]) + dot(dense[2], blocks[2])


def forward_last_body(dense, b3, a3, most, to2, to3, to1, own, blocks, total):
    me = place()
    put_block(me, blocks, 0, a3, b3)
    total[...] = most[...] + dot(dense[3], blocks[0])
    for k, to in enumerate((own, to1, to2, to3)):
        to[...] = total[at(me["x"] ^ k, PART), :].astype(to.dtype)


def sum_body(own, r3, r1, r2, cot, to_h):
    total = own[...] + r1[...].astype(F32) + (r2[...].astype(F32) + r3[...].astype(F32))
    high, low = split(total)
    to_h[0:PART, :] = high
    to_h[PART : 2 * PART, :] = low
    to_h[2 * PART :, :] = cot[...]


def aggregate_of(mine, got):
    parts = [ref[0:PART, :].astype(F32) + ref[PART : 2 * PART, :].astype(F32) for ref in (mine, got)]
    return (parts[0] + parts[1]).astype(BF)


def layer_body(mine, got, weight, to2, to3, to1, own, aggregate, share, grad_w):
    me = place()
    agg = aggregate_of(mine, got)
    preact = dot(agg, weight[...])
    gates = jax.nn.sigmoid(preact)
    first = me["h"] == 0
    a, b = mine[2 * PART :, :], got[2 * PART :, :]
    cotangent = jnp.concatenate([jnp.where(first, a, b), jnp.where(first, b, a)], axis=0).astype(F32)
    grad_pre = (cotangent * gates * (1.0 + preact * (1.0 - gates))).astype(BF)
    grad_w[...] = dot(agg, grad_pre, ((0,), (0,)))
    aggregate[...] = agg
    own[...] = grad_pre
    share[...] = grad_w[at(me["x"], SLICE), :]
    for k, to in ((3, to3), (2, to2), (1, to1)):
        to[0:PART, :] = grad_pre
        to[PART:, :] = grad_w[at(me["x"] ^ k, SLICE), :].astype(BF)


def output_body(aggregate, weight, output):
    preact = dot(aggregate[at(place()["h"], SLICE), :], weight[...])
    output[...] = (preact * jax.nn.sigmoid(preact)).astype(BF)


def backward_body(dense_t, weight, m0, m2, m3, m1, share, to_c, grad_agg, grad_pre):
    me = place()
    for k, m in enumerate((m0, m1, m2, m3)):
        grad_pre[at(me["x"] ^ k, PART), :] = m[0:PART, :]
    grad = dot(grad_pre[...], weight[...], ((1,), (1,))).astype(BF)
    grad_agg[...] = grad
    to_c[0:BLOCK, :] = dot(dense_t[3], grad)
    total = share[...] + m1[PART:, :].astype(F32)
    to_c[BLOCK:, :] = total + (m2[PART:, :].astype(F32) + m3[PART:, :].astype(F32))


def keep_body(dense_t, grad_agg, keep):
    keep[...] = dot(dense_t[2], grad_agg[...])


def to_u_body(keep, mine, got, u3, u2, u1, u0, share):
    me = place()
    for k, out in ((3, u3), (2, u2), (1, u1), (0, u0)):
        rows = at(me["z"] ^ k, PART)
        out[0:PART, :] = (keep[rows, :] + got[rows, :]).astype(BF)
    both = (mine[BLOCK:, :] + got[BLOCK:, :]).astype(BF)
    u3[PART:, :] = both
    share[...] = both


def kept_body(dense_t, grad_agg, to_c, keep):
    to_c[...] = dot(dense_t[1], grad_agg[...])
    keep[...] = dot(dense_t[0], grad_agg[...])


def after_c_body(keep, got, own, total):
    me = place()
    total[...] = keep[...] + got[...]
    for k in range(4):
        own[k * PART : (k + 1) * PART, :] = total[at(me["z"] ^ k, PART), :]


def to_z_body(k, own, got, to):
    to[...] = (own[k * PART : (k + 1) * PART, :] + got[0:PART, :].astype(F32)).astype(BF)


def to_z3_body(own, got, to):
    to_z_body(3, own, got, to)


def to_z2_body(own, got, earlier, to):
    to_z_body(2, own, got, to)


def to_z1_body(own, got, got_own, share, earlier, to, kept, total):
    to_z_body(1, own, got, to)
    kept[...] = own[0:PART, :] + got_own[...].astype(F32)
    total[...] = share[...].astype(F32) + earlier[PART:, :].astype(F32)


def after_z_body(kept, r1, r2, r3, mine, got, to_v, share):
    total = kept[...] + r1[...].astype(F32)
    to_v[...] = total + (r2[...].astype(F32) + r3[...].astype(F32))
    share[...] = mine[...] + got[...]


def after_v_body(one, two, mine, got, piece, share):
    piece[...] = (one[...] + two[...]).astype(BF)
    share[...] = mine[...] + got[...]


def last_body(piece, mine, got, message):
    message[0:PART, :] = piece[...]
    put_split(message, PART, mine[...] + got[...])


def finish_body(m0, m2, m3, m1, grad_features, grad_weight):
    me = place()
    for k, message in enumerate((m0, m1, m2, m3)):
        grad_features[at(chunk_of(me, me["x"] ^ k), PART), :] = message[0:PART, :]
        grad_weight[at(me["x"] ^ k, SLICE), :] = get_split(message, PART)


def on_device(features, weight, cotangent, tile_values, tile_slots, tile_count):
    part = ((PART, WIDTH), BF)
    part32 = ((PART, WIDTH), F32)
    block = ((BLOCK, WIDTH), BF)
    block32 = ((BLOCK, WIDTH), F32)
    share32 = ((SLICE, WIDTH), F32)
    share16 = ((SLICE, WIDTH), BF)
    two = ((2 * PART, WIDTH), BF)
    to_z = ((PART + SLICE, WIDTH), BF)
    dense_shape = ((4, BLOCK, BLOCK), BF)

    (half,) = call(half_body, [two], features, specs=[HBM], scratch=[pltpu.SemaphoreType.DMA])
    half = send(half, TO_COLUMN)
    dense, dense_t = call(
        dense_body, [dense_shape, dense_shape], tile_slots, tile_count, tile_values, specs=[SMEM, SMEM, VMEM]
    )
    half, dense, dense_t = lax.optimization_barrier((half, dense, dense_t))
    mine = [half, send(half, FLIP_Z[0])]
    by_u = [send(value, FLIP_U) for value in mine]
    by_c = [send(value, FLIP_C) for value in mine]
    by_uc = [send(value, FLIP_C) for value in by_u]
    total = pltpu.VMEM((BLOCK, WIDTH), F32)
    (most,) = call(
        forward_body, [block32], dense, *mine[::-1], *by_c[::-1], *by_u[::-1], scratch=[pltpu.VMEM((3, BLOCK, WIDTH), BF)]
    )
    *to, own = call(
        forward_last_body, [part, part, part, part32], dense, *by_uc[::-1], most, scratch=[pltpu.VMEM((1, BLOCK, WIDTH), BF), total]
    )
    got = [send(value, route) for value, route in zip(to, FAR_X)]
    (mine,) = call(sum_body, [((2 * PART + SLICE, WIDTH), BF)], own, got[1], got[2], got[0], cotangent)
    got = send(mine, FLIP_H)
    *to, own, aggregate, share = call(
        layer_body, [to_z, to_z, to_z, part, part, share32], mine, got, weight, scratch=[pltpu.VMEM((WIDTH, WIDTH), F32)]
    )
    (output,) = call(output_body, [((SLICE, WIDTH), BF)], aggregate, weight)
    got = [send(value, route) for value, route in zip(to, FAR_X)]
    to_c, grad_agg = call(
        backward_body, [((BLOCK + SLICE, WIDTH), F32), block], dense_t, weight, own, *got, share,
        scratch=[pltpu.VMEM((BLOCK, WIDTH), BF)],
    )
    got = send(to_c, FLIP_C)
    (keep_u,) = call(keep_body, [block32], dense_t, grad_agg)
    *to_u, share = call(to_u_body, [to_z, part, part, part, share16], keep_u, to_c, got)
    u3, u2, u1, u0 = [send(value, FLIP_U) for value in to_u]
    to_c, keep = call(kept_body, [block32, block32], dense_t, grad_agg)
    (own,) = call(after_c_body, [block32], keep, send(to_c, FLIP_C), scratch=[total])
    (to3,) = call(to_z3_body, [part], own, u3)
    (to2,) = call(to_z2_body, [part], own, u2, u3)
    to1, kept, share = call(to_z1_body, [part, part32, share32], own, u1, u0, share, u3)
    from_z = [send(value, route) for value, route in zip((to1, to2, to3), FLIP_Z)]
    to_v, share = call(after_z_body, [part32, share32], kept, *from_z, share, send(share, FLIP_Z[0]))
    piece, share = call(
        after_v_body, [part, share32], to_v, send(to_v, FLIP_V), share, send(share, FLIP_Z[1])
    )
    (message,) = call(last_body, [two], send(piece, TO_ROW), share, send(share, FLIP_V))
    grad_features, grad_weight = call(finish_body, [block, ((WIDTH, WIDTH), F32)], message, *[send(message, route) for route in FAR_X])
    return output, grad_weight, grad_features


def solution(mesh):
    placed = (
        P("rows", None),
        P(),
        P(("rows", "rep"), None),
        P("rows", "rep", None, None, None),
        P("rows", "rep", None),
        P("rows", "rep"),
    )
    return jax.shard_map(
        on_device,
        mesh=mesh,
        in_specs=placed,
        out_specs=(P(("rows", "rep"), None), P(), P("rows", None)),
        check_vma=False,
    )
```

```python
import itertools

import jax
import jax.numpy as jnp
from jax import lax
from jax.experimental import pallas as pl
from jax.experimental.pallas import tpu as pltpu
from jax.sharding import PartitionSpec as P

BF = jnp.bfloat16
F32 = jnp.float32
TILE = 128
WIDTH = 256
BLOCK = 512
PART = 128
SLICE = 64
AXES = ("rows", "rep")


def u_of(y):
    return (y ^ (y >> 1)) & 1


def v_of(y):
    return y >> 1


Y_OF = {(u_of(y), v_of(y)): y for y in range(4)}
PLACES = list(itertools.product(range(4), range(4), range(2), range(4), range(2)))


def index_of(z, y, c, x, h):
    return (z * 8 + y * 2 + c) * 8 + x * 2 + h


def pairs(target):
    return [(index_of(*place), index_of(*target(*place))) for place in PLACES]


FLIP_C = pairs(lambda z, y, c, x, h: (z, y, 1 - c, x, h))
FLIP_U = pairs(lambda z, y, c, x, h: (z, Y_OF[1 - u_of(y), v_of(y)], c, x, h))
FLIP_V = pairs(lambda z, y, c, x, h: (z, Y_OF[u_of(y), 1 - v_of(y)], c, x, h))
FLIP_H = pairs(lambda z, y, c, x, h: (z, y, c, x, 1 - h))
FLIP_X = [pairs(lambda z, y, c, x, h, k=k: (z, y, c, x ^ k, h)) for k in (1, 2, 3)]
FLIP_Z = [pairs(lambda z, y, c, x, h, k=k: (z ^ k, y, c, x, h)) for k in (1, 2, 3)]
FAR_X = (FLIP_X[1], FLIP_X[2], FLIP_X[0])
ROUTE = (((2, 1, 3, 0), (0, 3, 2, 1), (2, 1, 0, 3), (3, 0, 2, 1)), ((0, 1, 3, 2), (0, 1, 2, 3), (0, 1, 2, 3), (1, 0, 2, 3)))
TO_ROW = pairs(lambda z, y, c, x, h: (x, Y_OF[u_of(y), h], c, ROUTE[v_of(y) == h][x][z], 1 - v_of(y)))
SERVED = (
    (6, 0, 4, 2, 5, 3, 1, 7), (2, 4, 0, 6, 5, 1, 3, 7), (2, 0, 4, 6, 5, 1, 3, 7), (6, 4, 0, 2, 7, 3, 1, 5),
    (5, 3, 1, 7, 0, 4, 6, 2), (5, 7, 3, 1, 6, 2, 4, 0), (1, 7, 3, 5, 0, 4, 6, 2), (5, 3, 7, 1, 2, 6, 4, 0),
    (5, 3, 6, 4, 0, 2, 7, 1), (5, 3, 0, 2, 4, 6, 7, 1), (2, 3, 4, 0, 1, 6, 7, 5), (5, 3, 0, 6, 2, 4, 7, 1),
    (1, 5, 3, 7, 2, 4, 0, 6), (2, 4, 7, 3, 5, 1, 0, 6), (2, 4, 7, 5, 1, 3, 0, 6), (2, 5, 1, 3, 7, 4, 0, 6),
    (1, 7, 4, 6, 2, 0, 3, 5), (1, 7, 2, 0, 6, 4, 3, 5), (1, 7, 0, 2, 4, 6, 3, 5), (1, 7, 4, 5, 6, 2, 3, 0),
    (2, 0, 4, 6, 5, 1, 7, 3), (6, 0, 7, 5, 1, 3, 4, 2), (6, 0, 4, 7, 5, 1, 3, 2), (6, 0, 3, 1, 5, 7, 4, 2),
    (7, 1, 3, 5, 6, 4, 0, 2), (5, 3, 7, 1, 0, 6, 4, 2), (5, 3, 7, 1, 6, 0, 4, 2), (7, 1, 3, 5, 2, 4, 0, 6),
    (6, 4, 0, 2, 3, 1, 7, 5), (0, 6, 4, 2, 7, 5, 3, 1), (2, 4, 0, 6, 3, 5, 7, 1), (0, 6, 4, 2, 7, 1, 3, 5),
)


def served(z, y, c, x, h):
    replica = SERVED[x * 8 + h * 4 + u_of(y) * 2 + c][z * 2 + v_of(y)]
    return x, Y_OF[u_of(y), h], c, replica >> 1, replica & 1


TO_COLUMN = [(there, here) for here, there in pairs(served)]


def half_words():
    words = [0] * 8
    for there, here in TO_COLUMN:
        words[there >> 5] |= (here >> 6 & 1) << (there & 31)
    return [word - (1 << 32) if word >> 31 else word for word in words]


HALVES = half_words()


def chunk_table(same):
    word = sum((z << (8 * x + 2 * ROUTE[same][x][z])) for x in range(4) for z in range(4))
    return word - (1 << 32) if word >> 31 else word


CHUNKS = (chunk_table(0), chunk_table(1))


def send(value, route):
    return lax.ppermute(value, AXES, route)


def place():
    r = lax.axis_index("rows")
    p = lax.axis_index("rep")
    y = (r >> 1) & 3
    v = y >> 1
    return dict(z=r >> 3, c=r & 1, u=(y ^ v) & 1, v=v, x=p >> 1, h=p & 1)


def chunk_of(me, x):
    word = jnp.where((1 - me["h"]) == me["v"], jnp.int32(CHUNKS[1]), jnp.int32(CHUNKS[0]))
    return (word >> (8 * me["z"] + 2 * x)) & 3


def at(index, size):
    return pl.ds(pl.multiple_of(index * size, size), size)


def dot(a, b, dims=((1,), (0,))):
    return lax.dot_general(a, b, (dims, ((), ())), preferred_element_type=F32)


SMEM = pl.BlockSpec(memory_space=pltpu.SMEM)
VMEM = pl.BlockSpec(memory_space=pltpu.VMEM)
HBM = pl.BlockSpec(memory_space=pl.ANY)


def call(body, outs, *args, specs=None, scratch=()):
    return pl.pallas_call(
        body,
        out_shape=[jax.ShapeDtypeStruct(shape, dtype) for shape, dtype in outs],
        in_specs=specs or [VMEM] * len(args),
        out_specs=[VMEM] * len(outs),
        scratch_shapes=list(scratch),
        compiler_params=pltpu.CompilerParams(vmem_limit_bytes=24 * 2**20),
    )(*args)


def split(value):
    high = value.astype(BF)
    return high, (value - high.astype(F32)).astype(BF)


def put_split(ref, start, value):
    high, low = split(value)
    ref[start : start + SLICE, :] = high
    ref[start + SLICE : start + 2 * SLICE, :] = low


def get_split(ref, start):
    return ref[start : start + SLICE, :].astype(F32) + ref[start + SLICE : start + 2 * SLICE, :].astype(F32)


def half_body(features, out, sem):
    device = lax.axis_index("rows") * 8 + lax.axis_index("rep")
    word = jnp.int32(0)
    for i, value in enumerate(HALVES):
        word = jnp.where(device >> 5 == i, jnp.int32(value), word)
    half = (word >> (device & 31)) & 1
    copy = pltpu.make_async_copy(features.at[at(half, 2 * PART), :], out, sem)
    copy.start()
    copy.wait()


def dense_body(slots, count, tiles, dense, dense_t):
    me = place()
    dense[...] = jnp.zeros_like(dense)
    dense_t[...] = jnp.zeros_like(dense_t)
    for k in range(4):
        b = ((me["u"] ^ me["h"]) * 2 + me["c"]) ^ k
        for s in range(2):
            slot = slots[0, b, s]
            tile = jnp.where(s < count[0, b], tiles[0, b, s], jnp.zeros((), BF))

            @pl.when(s < count[0, b])
            def _():
                dense[k, at(slot >> 2, TILE), at(slot & 3, TILE)] = tile
                dense_t[k, at(slot & 3, TILE), at(slot >> 2, TILE)] = tile.T


def put_block(me, blocks, i, mine, other):
    half = me["z"] & 1
    blocks[i, at(half, 2 * PART), :] = mine[...]
    blocks[i, at(1 - half, 2 * PART), :] = other[...]


def forward_body(dense, b0, a0, b1, a1, b2, a2, total, blocks):
    me = place()
    for i, (first, second) in enumerate(((a0, b0), (a1, b1), (a2, b2))):
        put_block(me, blocks, i, first, second)
    total[...] = dot(dense[0], blocks[0]) + dot(dense[1], blocks[1]) + dot(dense[2], blocks[2])


def forward_last_body(dense, b3, a3, most, to2, to3, to1, own, blocks, total):
    me = place()
    put_block(me, blocks, 0, a3, b3)
    total[...] = most[...] + dot(dense[3], blocks[0])
    for k, to in enumerate((own, to1, to2, to3)):
        to[...] = total[at(me["x"] ^ k, PART), :].astype(to.dtype)


def sum_body(own, r3, r1, r2, cot, to_h):
    total = own[...] + r1[...].astype(F32) + (r2[...].astype(F32) + r3[...].astype(F32))
    high, low = split(total)
    to_h[0:PART, :] = high
    to_h[PART : 2 * PART, :] = low
    to_h[2 * PART :, :] = cot[...]


def aggregate_of(mine, got):
    parts = [ref[0:PART, :].astype(F32) + ref[PART : 2 * PART, :].astype(F32) for ref in (mine, got)]
    return (parts[0] + parts[1]).astype(BF)


def layer_body(mine, got, weight, to2, to3, to1, own, aggregate, share, grad_w):
    me = place()
    agg = aggregate_of(mine, got)
    preact = dot(agg, weight[...])
    gates = jax.nn.sigmoid(preact)
    first = me["h"] == 0
    a, b = mine[2 * PART :, :], got[2 * PART :, :]
    cotangent = jnp.concatenate([jnp.where(first, a, b), jnp.where(first, b, a)], axis=0).astype(F32)
    grad_pre = (cotangent * gates * (1.0 + preact * (1.0 - gates))).astype(BF)
    grad_w[...] = dot(agg, grad_pre, ((0,), (0,)))
    aggregate[...] = agg
    own[...] = grad_pre
    share[...] = grad_w[at(me["x"], SLICE), :]
    for k, to in ((3, to3), (2, to2), (1, to1)):
        to[0:PART, :] = grad_pre
        to[PART:, :] = grad_w[at(me["x"] ^ k, SLICE), :].astype(BF)


def output_body(aggregate, weight, output):
    preact = dot(aggregate[at(place()["h"], SLICE), :], weight[...])
    output[...] = (preact * jax.nn.sigmoid(preact)).astype(BF)


def backward_body(dense_t, weight, m0, m2, m3, m1, share, to_c, grad_agg, grad_pre):
    me = place()
    for k, m in enumerate((m0, m1, m2, m3)):
        grad_pre[at(me["x"] ^ k, PART), :] = m[0:PART, :]
    grad = dot(grad_pre[...], weight[...], ((1,), (1,))).astype(BF)
    grad_agg[...] = grad
    to_c[0:BLOCK, :] = dot(dense_t[3], grad)
    total = share[...] + m1[PART:, :].astype(F32)
    to_c[BLOCK:, :] = total + (m2[PART:, :].astype(F32) + m3[PART:, :].astype(F32))


def keep_body(dense_t, grad_agg, keep):
    keep[...] = dot(dense_t[2], grad_agg[...])


def to_u_body(keep, mine, got, u3, u2, u1, u0, share):
    me = place()
    for k, out in ((3, u3), (2, u2), (1, u1), (0, u0)):
        rows = at(me["z"] ^ k, PART)
        out[0:PART, :] = (keep[rows, :] + got[rows, :]).astype(BF)
    both = (mine[BLOCK:, :] + got[BLOCK:, :]).astype(BF)
    u3[PART:, :] = both
    share[...] = both


def kept_body(dense_t, grad_agg, to_c, keep):
    to_c[...] = dot(dense_t[1], grad_agg[...])
    keep[...] = dot(dense_t[0], grad_agg[...])


def after_c_body(keep, got, own, total):
    me = place()
    total[...] = keep[...] + got[...]
    for k in range(4):
        own[k * PART : (k + 1) * PART, :] = total[at(me["z"] ^ k, PART), :]


def to_z_body(k, own, got, to):
    to[...] = (own[k * PART : (k + 1) * PART, :] + got[0:PART, :].astype(F32)).astype(BF)


def to_z3_body(own, got, to):
    to_z_body(3, own, got, to)


def to_z2_body(own, got, earlier, to):
    to_z_body(2, own, got, to)


def to_z1_body(own, got, got_own, share, earlier, to, kept, total):
    to_z_body(1, own, got, to)
    kept[...] = own[0:PART, :] + got_own[...].astype(F32)
    total[...] = share[...].astype(F32) + earlier[PART:, :].astype(F32)


def after_z_body(kept, r1, r2, r3, mine, got, to_v, share):
    total = kept[...] + r1[...].astype(F32)
    to_v[...] = total + (r2[...].astype(F32) + r3[...].astype(F32))
    share[...] = mine[...] + got[...]


def after_v_body(one, two, mine, got, piece, share):
    piece[...] = (one[...] + two[...]).astype(BF)
    share[...] = mine[...] + got[...]


def last_body(piece, mine, got, message):
    message[0:PART, :] = piece[...]
    put_split(message, PART, mine[...] + got[...])


def finish_body(m0, m2, m3, m1, grad_features, grad_weight):
    me = place()
    for k, message in enumerate((m0, m1, m2, m3)):
        grad_features[at(chunk_of(me, me["x"] ^ k), PART), :] = message[0:PART, :]
        grad_weight[at(me["x"] ^ k, SLICE), :] = get_split(message, PART)


def on_device(features, weight, cotangent, tile_values, tile_slots, tile_count):
    part = ((PART, WIDTH), BF)
    part32 = ((PART, WIDTH), F32)
    block = ((BLOCK, WIDTH), BF)
    block32 = ((BLOCK, WIDTH), F32)
    share32 = ((SLICE, WIDTH), F32)
    share16 = ((SLICE, WIDTH), BF)
    two = ((2 * PART, WIDTH), BF)
    to_z = ((PART + SLICE, WIDTH), BF)
    dense_shape = ((4, BLOCK, BLOCK), BF)

    (half,) = call(half_body, [two], features, specs=[HBM], scratch=[pltpu.SemaphoreType.DMA])
    half = send(half, TO_COLUMN)
    dense, dense_t = call(
        dense_body, [dense_shape, dense_shape], tile_slots, tile_count, tile_values, specs=[SMEM, SMEM, VMEM]
    )
    half, dense, dense_t = lax.optimization_barrier((half, dense, dense_t))
    mine = [half, send(half, FLIP_Z[0])]
    by_u = [send(value, FLIP_U) for value in mine]
    by_c = [send(value, FLIP_C) for value in mine]
    by_uc = [send(value, FLIP_C) for value in by_u]
    total = pltpu.VMEM((BLOCK, WIDTH), F32)
    (most,) = call(
        forward_body, [block32], dense, *mine[::-1], *by_c[::-1], *by_u[::-1], scratch=[pltpu.VMEM((3, BLOCK, WIDTH), BF)]
    )
    *to, own = call(
        forward_last_body, [part, part, part, part32], dense, *by_uc[::-1], most, scratch=[pltpu.VMEM((1, BLOCK, WIDTH), BF), total]
    )
    got = [send(value, route) for value, route in zip(to, FAR_X)]
    (mine,) = call(sum_body, [((2 * PART + SLICE, WIDTH), BF)], own, got[1], got[2], got[0], cotangent)
    got = send(mine, FLIP_H)
    *to, own, aggregate, share = call(
        layer_body, [to_z, to_z, to_z, part, part, share32], mine, got, weight, scratch=[pltpu.VMEM((WIDTH, WIDTH), F32)]
    )
    (output,) = call(output_body, [((SLICE, WIDTH), BF)], aggregate, weight)
    got = [send(value, route) for value, route in zip(to, FAR_X)]
    to_c, grad_agg = call(
        backward_body, [((BLOCK + SLICE, WIDTH), F32), block], dense_t, weight, own, *got, share,
        scratch=[pltpu.VMEM((BLOCK, WIDTH), BF)],
    )
    got = send(to_c, FLIP_C)
    (keep_u,) = call(keep_body, [block32], dense_t, grad_agg)
    *to_u, share = call(to_u_body, [to_z, part, part, part, share16], keep_u, to_c, got)
    u3, u2, u1, u0 = [send(value, FLIP_U) for value in to_u]
    to_c, keep = call(kept_body, [block32, block32], dense_t, grad_agg)
    (own,) = call(after_c_body, [block32], keep, send(to_c, FLIP_C), scratch=[total])
    (to3,) = call(to_z3_body, [part], own, u3)
    (to2,) = call(to_z2_body, [part], own, u2, u3)
    to1, kept, share = call(to_z1_body, [part, part32, share32], own, u1, u0, share, u3)
    from_z = [send(value, route) for value, route in zip((to1, to2, to3), FLIP_Z)]
    to_v, share = call(after_z_body, [part32, share32], kept, *from_z, share, send(share, FLIP_Z[0]))
    piece, share = call(
        after_v_body, [part, share32], to_v, send(to_v, FLIP_V), share, send(share, FLIP_Z[1])
    )
    (message,) = call(last_body, [two], send(piece, TO_ROW), share, send(share, FLIP_V))
    grad_features, grad_weight = call(finish_body, [block, ((WIDTH, WIDTH), F32)], message, *[send(message, route) for route in FAR_X])
    return output, grad_weight, grad_features


def solution(mesh):
    placed = (
        P("rows", None),
        P(),
        P(("rows", "rep"), None),
        P("rows", "rep", None, None, None),
        P("rows", "rep", None),
        P("rows", "rep"),
    )
    return jax.shard_map(
        on_device,
        mesh=mesh,
        in_specs=placed,
        out_specs=(P(("rows", "rep"), None), P(), P("rows", None)),
        check_vma=False,
    )
```

```python
import itertools

import jax
import jax.numpy as jnp
from jax import lax
from jax.experimental import pallas as pl
from jax.experimental.pallas import tpu as pltpu
from jax.sharding import PartitionSpec as P

BF = jnp.bfloat16
F32 = jnp.float32
TILE = 128
WIDTH = 256
BLOCK = 512
PART = 128
SLICE = 64
AXES = ("rows", "rep")


def u_of(y):
    return (y ^ (y >> 1)) & 1


def v_of(y):
    return y >> 1


Y_OF = {(u_of(y), v_of(y)): y for y in range(4)}
PLACES = list(itertools.product(range(4), range(4), range(2), range(4), range(2)))


def index_of(z, y, c, x, h):
    return (z * 8 + y * 2 + c) * 8 + x * 2 + h


def pairs(target):
    return [(index_of(*place), index_of(*target(*place))) for place in PLACES]


FLIP_C = pairs(lambda z, y, c, x, h: (z, y, 1 - c, x, h))
FLIP_U = pairs(lambda z, y, c, x, h: (z, Y_OF[1 - u_of(y), v_of(y)], c, x, h))
FLIP_V = pairs(lambda z, y, c, x, h: (z, Y_OF[u_of(y), 1 - v_of(y)], c, x, h))
FLIP_H = pairs(lambda z, y, c, x, h: (z, y, c, x, 1 - h))
FLIP_X = [pairs(lambda z, y, c, x, h, k=k: (z, y, c, x ^ k, h)) for k in (1, 2, 3)]
FLIP_Z = [pairs(lambda z, y, c, x, h, k=k: (z ^ k, y, c, x, h)) for k in (1, 2, 3)]
FAR_X = (FLIP_X[1], FLIP_X[2], FLIP_X[0])
ROUTE = (((2, 1, 3, 0), (0, 3, 2, 1), (2, 1, 0, 3), (3, 0, 2, 1)), ((0, 1, 3, 2), (0, 1, 2, 3), (0, 1, 2, 3), (1, 0, 2, 3)))
TO_ROW = pairs(lambda z, y, c, x, h: (x, Y_OF[u_of(y), h], c, ROUTE[v_of(y) == h][x][z], 1 - v_of(y)))
SERVED = (
    (2, 4, 0, 6, 5, 3, 1, 7), (2, 4, 0, 6, 5, 3, 1, 7), (6, 0, 4, 2, 5, 3, 1, 7), (6, 0, 4, 2, 5, 3, 1, 7),
    (5, 3, 7, 1, 2, 4, 6, 0), (5, 3, 7, 1, 2, 4, 6, 0), (1, 7, 5, 3, 2, 4, 6, 0), (1, 7, 5, 3, 2, 4, 6, 0),
    (5, 3, 4, 2, 0, 6, 7, 1), (5, 3, 4, 2, 0, 6, 7, 1), (5, 3, 0, 6, 2, 4, 7, 1), (5, 3, 0, 6, 2, 4, 7, 1),
    (2, 4, 3, 5, 7, 1, 0, 6), (2, 4, 3, 5, 7, 1, 0, 6), (2, 4, 3, 5, 7, 1, 0, 6), (2, 4, 3, 5, 7, 1, 0, 6),
    (1, 7, 6, 0, 2, 4, 3, 5), (1, 7, 6, 0, 2, 4, 3, 5), (1, 7, 6, 4, 2, 0, 3, 5), (1, 7, 6, 4, 2, 0, 3, 5),
    (6, 0, 1, 7, 5, 3, 4, 2), (6, 0, 1, 7, 5, 3, 4, 2), (6, 0, 7, 1, 5, 3, 4, 2), (6, 0, 7, 1, 5, 3, 4, 2),
    (7, 1, 3, 5, 6, 0, 4, 2), (7, 1, 3, 5, 6, 0, 4, 2), (5, 3, 7, 1, 0, 6, 4, 2), (5, 3, 7, 1, 0, 6, 4, 2),
    (0, 6, 4, 2, 1, 7, 3, 5), (0, 6, 4, 2, 1, 7, 3, 5), (2, 4, 0, 6, 1, 7, 3, 5), (2, 4, 0, 6, 1, 7, 3, 5),
)


def served(z, y, c, x, h):
    replica = SERVED[x * 8 + h * 4 + u_of(y) * 2 + c][z * 2 + v_of(y)]
    return x, Y_OF[u_of(y), h], c, replica >> 1, replica & 1


TO_COLUMN = [(there, here) for here, there in pairs(served)]


def half_words():
    words = [0] * 8
    for there, here in TO_COLUMN:
        words[there >> 5] |= (here >> 6 & 1) << (there & 31)
    return [word - (1 << 32) if word >> 31 else word for word in words]


HALVES = half_words()


def chunk_table(same):
    word = sum((z << (8 * x + 2 * ROUTE[same][x][z])) for x in range(4) for z in range(4))
    return word - (1 << 32) if word >> 31 else word


CHUNKS = (chunk_table(0), chunk_table(1))


def send(value, route):
    return lax.ppermute(value, AXES, route)


def place():
    r = lax.axis_index("rows")
    p = lax.axis_index("rep")
    y = (r >> 1) & 3
    v = y >> 1
    return dict(z=r >> 3, c=r & 1, u=(y ^ v) & 1, v=v, x=p >> 1, h=p & 1)


def chunk_of(me, x):
    word = jnp.where((1 - me["h"]) == me["v"], jnp.int32(CHUNKS[1]), jnp.int32(CHUNKS[0]))
    return (word >> (8 * me["z"] + 2 * x)) & 3


def at(index, size):
    return pl.ds(pl.multiple_of(index * size, size), size)


def dot(a, b, dims=((1,), (0,))):
    return lax.dot_general(a, b, (dims, ((), ())), preferred_element_type=F32)


SMEM = pl.BlockSpec(memory_space=pltpu.SMEM)
VMEM = pl.BlockSpec(memory_space=pltpu.VMEM)
HBM = pl.BlockSpec(memory_space=pl.ANY)


def call(body, outs, *args, specs=None, scratch=()):
    return pl.pallas_call(
        body,
        out_shape=[jax.ShapeDtypeStruct(shape, dtype) for shape, dtype in outs],
        in_specs=specs or [VMEM] * len(args),
        out_specs=[VMEM] * len(outs),
        scratch_shapes=list(scratch),
        compiler_params=pltpu.CompilerParams(vmem_limit_bytes=24 * 2**20),
    )(*args)


def split(value):
    high = value.astype(BF)
    return high, (value - high.astype(F32)).astype(BF)


def put_split(ref, start, value):
    high, low = split(value)
    ref[start : start + SLICE, :] = high
    ref[start + SLICE : start + 2 * SLICE, :] = low


def get_split(ref, start):
    return ref[start : start + SLICE, :].astype(F32) + ref[start + SLICE : start + 2 * SLICE, :].astype(F32)


def half_body(features, out, sem):
    device = lax.axis_index("rows") * 8 + lax.axis_index("rep")
    word = jnp.int32(0)
    for i, value in enumerate(HALVES):
        word = jnp.where(device >> 5 == i, jnp.int32(value), word)
    half = (word >> (device & 31)) & 1
    copy = pltpu.make_async_copy(features.at[at(half, 2 * PART), :], out, sem)
    copy.start()
    copy.wait()


def dense_body(slots, count, tiles, dense, dense_t):
    me = place()
    dense[...] = jnp.zeros_like(dense)
    dense_t[...] = jnp.zeros_like(dense_t)
    for k in range(4):
        b = ((me["u"] ^ me["h"]) * 2 + me["c"]) ^ k
        for s in range(2):
            slot = slots[0, b, s]
            tile = jnp.where(s < count[0, b], tiles[0, b, s], jnp.zeros((), BF))

            @pl.when(s < count[0, b])
            def _():
                dense[k, at(slot >> 2, TILE), at(slot & 3, TILE)] = tile
                dense_t[k, at(slot & 3, TILE), at(slot >> 2, TILE)] = tile.T


def put_block(me, blocks, i, mine, other):
    half = me["z"] & 1
    blocks[i, at(half, 2 * PART), :] = mine[...]
    blocks[i, at(1 - half, 2 * PART), :] = other[...]


def forward_body(dense, b0, a0, b1, a1, b2, a2, total, blocks):
    me = place()
    for i, (first, second) in enumerate(((a0, b0), (a1, b1), (a2, b2))):
        put_block(me, blocks, i, first, second)
    total[...] = dot(dense[0], blocks[0]) + dot(dense[1], blocks[1]) + dot(dense[2], blocks[2])


def forward_last_body(dense, b3, a3, most, to2, to3, to1, own, blocks, total):
    me = place()
    put_block(me, blocks, 0, a3, b3)
    total[...] = most[...] + dot(dense[3], blocks[0])
    for k, to in enumerate((own, to1, to2, to3)):
        to[...] = total[at(me["x"] ^ k, PART), :].astype(to.dtype)


def sum_body(own, r3, r1, r2, cot, to_h):
    total = own[...] + r1[...].astype(F32) + (r2[...].astype(F32) + r3[...].astype(F32))
    to_h[0:PART, :] = total.astype(BF)
    to_h[PART:, :] = cot[...]


def aggregate_of(mine, got):
    return (mine[0:PART, :].astype(F32) + got[0:PART, :].astype(F32)).astype(BF)


def layer_body(mine, got, weight, to2, to3, to1, own, aggregate, share, grad_w):
    me = place()
    agg = aggregate_of(mine, got)
    preact = dot(agg, weight[...])
    gates = jax.nn.sigmoid(preact)
    first = me["h"] == 0
    a, b = mine[PART:, :], got[PART:, :]
    cotangent = jnp.concatenate([jnp.where(first, a, b), jnp.where(first, b, a)], axis=0).astype(F32)
    grad_pre = (cotangent * gates * (1.0 + preact * (1.0 - gates))).astype(BF)
    grad_w[...] = dot(agg, grad_pre, ((0,), (0,)))
    aggregate[...] = agg
    own[...] = grad_pre
    share[...] = grad_w[at(me["x"], SLICE), :]
    for k, to in ((3, to3), (2, to2), (1, to1)):
        to[0:PART, :] = grad_pre
        to[PART:, :] = grad_w[at(me["x"] ^ k, SLICE), :].astype(BF)


def output_body(aggregate, weight, output):
    preact = dot(aggregate[at(place()["h"], SLICE), :], weight[...])
    output[...] = (preact * jax.nn.sigmoid(preact)).astype(BF)


def backward_body(dense_t, weight, m0, m2, m3, m1, share, to_c, grad_agg, grad_pre):
    me = place()
    for k, m in enumerate((m0, m1, m2, m3)):
        grad_pre[at(me["x"] ^ k, PART), :] = m[0:PART, :]
    grad = dot(grad_pre[...], weight[...], ((1,), (1,))).astype(BF)
    grad_agg[...] = grad
    to_c[0:BLOCK, :] = dot(dense_t[3], grad)
    total = share[...] + m1[PART:, :].astype(F32)
    to_c[BLOCK:, :] = total + (m2[PART:, :].astype(F32) + m3[PART:, :].astype(F32))


def keep_body(dense_t, grad_agg, keep):
    keep[...] = dot(dense_t[2], grad_agg[...])


def to_u_body(keep, mine, got, u3, u2, u1, u0, share):
    me = place()
    for k, out in ((3, u3), (2, u2), (1, u1), (0, u0)):
        rows = at(me["z"] ^ k, PART)
        out[0:PART, :] = (keep[rows, :] + got[rows, :]).astype(BF)
    both = (mine[BLOCK:, :] + got[BLOCK:, :]).astype(BF)
    u3[PART:, :] = both
    share[...] = both


def kept_body(dense_t, grad_agg, to_c, keep):
    to_c[...] = dot(dense_t[1], grad_agg[...])
    keep[...] = dot(dense_t[0], grad_agg[...])


def after_c_body(keep, got, own, total):
    me = place()
    total[...] = keep[...] + got[...]
    for k in range(4):
        own[k * PART : (k + 1) * PART, :] = total[at(me["z"] ^ k, PART), :]


def to_z_body(k, own, got, to):
    to[...] = (own[k * PART : (k + 1) * PART, :] + got[0:PART, :].astype(F32)).astype(BF)


def to_z3_body(own, got, to):
    to_z_body(3, own, got, to)


def to_z2_body(own, got, earlier, to):
    to_z_body(2, own, got, to)


def to_z1_body(own, got, got_own, share, earlier, to, kept, total):
    to_z_body(1, own, got, to)
    kept[...] = own[0:PART, :] + got_own[...].astype(F32)
    total[...] = share[...].astype(F32) + earlier[PART:, :].astype(F32)


def after_z_body(kept, r1, r2, r3, mine, got, to_v, share):
    total = kept[...] + r1[...].astype(F32)
    to_v[...] = total + (r2[...].astype(F32) + r3[...].astype(F32))
    share[...] = mine[...] + got[...]


def after_v_body(one, two, mine, got, piece, share):
    piece[...] = (one[...] + two[...]).astype(BF)
    share[...] = mine[...] + got[...]


def last_body(piece, mine, got, message):
    message[0:PART, :] = piece[...]
    put_split(message, PART, mine[...] + got[...])


def finish_body(m0, m2, m3, m1, grad_features, grad_weight):
    me = place()
    for k, message in enumerate((m0, m1, m2, m3)):
        grad_features[at(chunk_of(me, me["x"] ^ k), PART), :] = message[0:PART, :]
        grad_weight[at(me["x"] ^ k, SLICE), :] = get_split(message, PART)


def on_device(features, weight, cotangent, tile_values, tile_slots, tile_count):
    part = ((PART, WIDTH), BF)
    part32 = ((PART, WIDTH), F32)
    block = ((BLOCK, WIDTH), BF)
    block32 = ((BLOCK, WIDTH), F32)
    share32 = ((SLICE, WIDTH), F32)
    share16 = ((SLICE, WIDTH), BF)
    two = ((2 * PART, WIDTH), BF)
    to_z = ((PART + SLICE, WIDTH), BF)
    dense_shape = ((4, BLOCK, BLOCK), BF)

    (half,) = call(half_body, [two], features, specs=[HBM], scratch=[pltpu.SemaphoreType.DMA])
    half = send(half, TO_COLUMN)
    dense, dense_t = call(
        dense_body, [dense_shape, dense_shape], tile_slots, tile_count, tile_values, specs=[SMEM, SMEM, VMEM]
    )
    half, dense, dense_t = lax.optimization_barrier((half, dense, dense_t))
    mine = [half, send(half, FLIP_Z[0])]
    by_u = [send(value, FLIP_U) for value in mine]
    by_c = [send(value, FLIP_C) for value in mine]
    by_uc = [send(value, FLIP_C) for value in by_u]
    total = pltpu.VMEM((BLOCK, WIDTH), F32)
    (most,) = call(
        forward_body, [block32], dense, *mine[::-1], *by_c[::-1], *by_u[::-1], scratch=[pltpu.VMEM((3, BLOCK, WIDTH), BF)]
    )
    *to, own = call(
        forward_last_body, [part, part, part, part32], dense, *by_uc[::-1], most, scratch=[pltpu.VMEM((1, BLOCK, WIDTH), BF), total]
    )
    got = [send(value, route) for value, route in zip(to, FAR_X)]
    (mine,) = call(sum_body, [to_z], own, got[1], got[2], got[0], cotangent)
    got = send(mine, FLIP_H)
    *to, own, aggregate, share = call(
        layer_body, [to_z, to_z, to_z, part, part, share32], mine, got, weight, scratch=[pltpu.VMEM((WIDTH, WIDTH), F32)]
    )
    (output,) = call(output_body, [((SLICE, WIDTH), BF)], aggregate, weight)
    got = [send(value, route) for value, route in zip(to, FAR_X)]
    to_c, grad_agg = call(
        backward_body, [((BLOCK + SLICE, WIDTH), F32), block], dense_t, weight, own, *got, share,
        scratch=[pltpu.VMEM((BLOCK, WIDTH), BF)],
    )
    got = send(to_c, FLIP_C)
    (keep_u,) = call(keep_body, [block32], dense_t, grad_agg)
    *to_u, share = call(to_u_body, [to_z, part, part, part, share16], keep_u, to_c, got)
    u3, u2, u1, u0 = [send(value, FLIP_U) for value in to_u]
    to_c, keep = call(kept_body, [block32, block32], dense_t, grad_agg)
    (own,) = call(after_c_body, [block32], keep, send(to_c, FLIP_C), scratch=[total])
    (to3,) = call(to_z3_body, [part], own, u3)
    (to2,) = call(to_z2_body, [part], own, u2, u3)
    to1, kept, share = call(to_z1_body, [part, part32, share32], own, u1, u0, share, u3)
    from_z = [send(value, route) for value, route in zip((to1, to2, to3), FLIP_Z)]
    to_v, share = call(after_z_body, [part32, share32], kept, *from_z, share, send(share, FLIP_Z[0]))
    piece, share = call(
        after_v_body, [part, share32], to_v, send(to_v, FLIP_V), share, send(share, FLIP_Z[1])
    )
    (message,) = call(last_body, [two], send(piece, TO_ROW), share, send(share, FLIP_V))
    grad_features, grad_weight = call(finish_body, [block, ((WIDTH, WIDTH), F32)], message, *[send(message, route) for route in FAR_X])
    return output, grad_weight, grad_features


def solution(mesh):
    placed = (
        P("rows", None),
        P(),
        P(("rows", "rep"), None),
        P("rows", "rep", None, None, None),
        P("rows", "rep", None),
        P("rows", "rep"),
    )
    return jax.shard_map(
        on_device,
        mesh=mesh,
        in_specs=placed,
        out_specs=(P(("rows", "rep"), None), P(), P("rows", None)),
        check_vma=False,
    )
```

```python
import itertools

import jax
import jax.numpy as jnp
from jax import lax
from jax.experimental import pallas as pl
from jax.experimental.pallas import tpu as pltpu
from jax.sharding import PartitionSpec as P

BF = jnp.bfloat16
F32 = jnp.float32
TILE = 128
WIDTH = 256
BLOCK = 512
PART = 128
SLICE = 64
PIECE = 16
AXES = ("rows", "rep")


def u_of(y):
    return (y ^ (y >> 1)) & 1


def v_of(y):
    return y >> 1


Y_OF = {(u_of(y), v_of(y)): y for y in range(4)}
PLACES = list(itertools.product(range(4), range(4), range(2), range(4), range(2)))


def index_of(z, y, c, x, h):
    return (z * 8 + y * 2 + c) * 8 + x * 2 + h


def pairs(target):
    return [(index_of(*place), index_of(*target(*place))) for place in PLACES]


FLIP_C = pairs(lambda z, y, c, x, h: (z, y, 1 - c, x, h))
FLIP_U = pairs(lambda z, y, c, x, h: (z, Y_OF[1 - u_of(y), v_of(y)], c, x, h))
FLIP_V = pairs(lambda z, y, c, x, h: (z, Y_OF[u_of(y), 1 - v_of(y)], c, x, h))
FLIP_H = pairs(lambda z, y, c, x, h: (z, y, c, x, 1 - h))
FLIP_X = [pairs(lambda z, y, c, x, h, k=k: (z, y, c, x ^ k, h)) for k in (1, 2, 3)]
FLIP_Z = [pairs(lambda z, y, c, x, h, k=k: (z ^ k, y, c, x, h)) for k in (1, 2, 3)]
FAR_X = (FLIP_X[1], FLIP_X[2], FLIP_X[0])
ROUTE = (((2, 1, 3, 0), (0, 3, 2, 1), (2, 1, 0, 3), (3, 0, 2, 1)), ((0, 1, 3, 2), (0, 1, 2, 3), (0, 1, 2, 3), (1, 0, 2, 3)))
TO_ROW = pairs(lambda z, y, c, x, h: (x, Y_OF[u_of(y), h], c, ROUTE[v_of(y) == h][x][z], 1 - v_of(y)))
SERVED = (
    (2, 4, 0, 6, 5, 3, 1, 7), (2, 4, 0, 6, 5, 3, 1, 7), (6, 0, 4, 2, 5, 3, 1, 7), (6, 0, 4, 2, 5, 3, 1, 7),
    (5, 3, 7, 1, 2, 4, 6, 0), (5, 3, 7, 1, 2, 4, 6, 0), (1, 7, 5, 3, 2, 4, 6, 0), (1, 7, 5, 3, 2, 4, 6, 0),
    (5, 3, 4, 2, 0, 6, 7, 1), (5, 3, 4, 2, 0, 6, 7, 1), (5, 3, 0, 6, 2, 4, 7, 1), (5, 3, 0, 6, 2, 4, 7, 1),
    (2, 4, 3, 5, 7, 1, 0, 6), (2, 4, 3, 5, 7, 1, 0, 6), (2, 4, 3, 5, 7, 1, 0, 6), (2, 4, 3, 5, 7, 1, 0, 6),
    (1, 7, 6, 0, 2, 4, 3, 5), (1, 7, 6, 0, 2, 4, 3, 5), (1, 7, 6, 4, 2, 0, 3, 5), (1, 7, 6, 4, 2, 0, 3, 5),
    (6, 0, 1, 7, 5, 3, 4, 2), (6, 0, 1, 7, 5, 3, 4, 2), (6, 0, 7, 1, 5, 3, 4, 2), (6, 0, 7, 1, 5, 3, 4, 2),
    (7, 1, 3, 5, 6, 0, 4, 2), (7, 1, 3, 5, 6, 0, 4, 2), (5, 3, 7, 1, 0, 6, 4, 2), (5, 3, 7, 1, 0, 6, 4, 2),
    (0, 6, 4, 2, 1, 7, 3, 5), (0, 6, 4, 2, 1, 7, 3, 5), (2, 4, 0, 6, 1, 7, 3, 5), (2, 4, 0, 6, 1, 7, 3, 5),
)


def served(z, y, c, x, h):
    replica = SERVED[x * 8 + h * 4 + u_of(y) * 2 + c][z * 2 + v_of(y)]
    return x, Y_OF[u_of(y), h], c, replica >> 1, replica & 1


TO_COLUMN = [(there, here) for here, there in pairs(served)]


def half_words():
    words = [0] * 8
    for there, here in TO_COLUMN:
        words[there >> 5] |= (here >> 6 & 1) << (there & 31)
    return [word - (1 << 32) if word >> 31 else word for word in words]


HALVES = half_words()


def chunk_table(same):
    word = sum((z << (8 * x + 2 * ROUTE[same][x][z])) for x in range(4) for z in range(4))
    return word - (1 << 32) if word >> 31 else word


CHUNKS = (chunk_table(0), chunk_table(1))


def send(value, route):
    return lax.ppermute(value, AXES, route)


def place():
    r = lax.axis_index("rows")
    p = lax.axis_index("rep")
    y = (r >> 1) & 3
    v = y >> 1
    return dict(z=r >> 3, c=r & 1, u=(y ^ v) & 1, v=v, x=p >> 1, h=p & 1)


def chunk_of(me, x):
    word = jnp.where((1 - me["h"]) == me["v"], jnp.int32(CHUNKS[1]), jnp.int32(CHUNKS[0]))
    return (word >> (8 * me["z"] + 2 * x)) & 3


def at(index, size):
    return pl.ds(pl.multiple_of(index * size, size), size)


def dot(a, b, dims=((1,), (0,))):
    return lax.dot_general(a, b, (dims, ((), ())), preferred_element_type=F32)


SMEM = pl.BlockSpec(memory_space=pltpu.SMEM)
VMEM = pl.BlockSpec(memory_space=pltpu.VMEM)
HBM = pl.BlockSpec(memory_space=pl.ANY)


def call(body, outs, *args, specs=None, scratch=()):
    return pl.pallas_call(
        body,
        out_shape=[jax.ShapeDtypeStruct(shape, dtype) for shape, dtype in outs],
        in_specs=specs or [VMEM] * len(args),
        out_specs=[VMEM] * len(outs),
        scratch_shapes=list(scratch),
        compiler_params=pltpu.CompilerParams(vmem_limit_bytes=24 * 2**20),
    )(*args)


def split(value):
    high = value.astype(BF)
    return high, (value - high.astype(F32)).astype(BF)


def put_split(ref, start, value):
    high, low = split(value)
    ref[start : start + SLICE, :] = high
    ref[start + SLICE : start + 2 * SLICE, :] = low


def get_split(ref, start):
    return ref[start : start + SLICE, :].astype(F32) + ref[start + SLICE : start + 2 * SLICE, :].astype(F32)


def half_body(features, out, sem):
    device = lax.axis_index("rows") * 8 + lax.axis_index("rep")
    word = jnp.int32(0)
    for i, value in enumerate(HALVES):
        word = jnp.where(device >> 5 == i, jnp.int32(value), word)
    half = (word >> (device & 31)) & 1
    copy = pltpu.make_async_copy(features.at[at(half, 2 * PART), :], out, sem)
    copy.start()
    copy.wait()


def dense_body(slots, count, tiles, dense, dense_t):
    me = place()
    dense[...] = jnp.zeros_like(dense)
    dense_t[...] = jnp.zeros_like(dense_t)
    for k in range(4):
        b = ((me["u"] ^ me["h"]) * 2 + me["c"]) ^ k
        for s in range(2):
            slot = slots[0, b, s]
            tile = jnp.where(s < count[0, b], tiles[0, b, s], jnp.zeros((), BF))

            @pl.when(s < count[0, b])
            def _():
                dense[k, at(slot >> 2, TILE), at(slot & 3, TILE)] = tile
                dense_t[k, at(slot & 3, TILE), at(slot >> 2, TILE)] = tile.T


def put_block(me, blocks, i, mine, other):
    half = me["z"] & 1
    blocks[i, at(half, 2 * PART), :] = mine[...]
    blocks[i, at(1 - half, 2 * PART), :] = other[...]


def forward_body(dense, b0, a0, b1, a1, b2, a2, total, blocks):
    me = place()
    for i, (first, second) in enumerate(((a0, b0), (a1, b1), (a2, b2))):
        put_block(me, blocks, i, first, second)
    total[...] = dot(dense[0], blocks[0]) + dot(dense[1], blocks[1]) + dot(dense[2], blocks[2])


def forward_last_body(dense, b3, a3, most, to2, to3, to1, own, blocks, total):
    me = place()
    put_block(me, blocks, 0, a3, b3)
    total[...] = most[...] + dot(dense[3], blocks[0])
    for k, to in enumerate((own, to1, to2, to3)):
        to[...] = total[at(me["x"] ^ k, PART), :].astype(to.dtype)


def sum_body(own, r3, r1, r2, cot, to_h):
    total = own[...] + r1[...].astype(F32) + (r2[...].astype(F32) + r3[...].astype(F32))
    to_h[0:PART, :] = total.astype(BF)
    to_h[PART:, :] = cot[...]


def aggregate_of(mine, got):
    return (mine[0:PART, :].astype(F32) + got[0:PART, :].astype(F32)).astype(BF)


def layer_body(mine, got, weight, to2, to3, to1, own, aggregate, share, grad_w):
    me = place()
    agg = aggregate_of(mine, got)
    preact = dot(agg, weight[...])
    gates = jax.nn.sigmoid(preact)
    first = me["h"] == 0
    a, b = mine[PART:, :], got[PART:, :]
    cotangent = jnp.concatenate([jnp.where(first, a, b), jnp.where(first, b, a)], axis=0).astype(F32)
    grad_pre = (cotangent * gates * (1.0 + preact * (1.0 - gates))).astype(BF)
    grad_w[...] = dot(agg, grad_pre, ((0,), (0,)))
    aggregate[...] = agg
    own[...] = grad_pre
    share[...] = grad_w[at(me["x"], SLICE), :]
    for k, to in ((3, to3), (2, to2), (1, to1)):
        to[0:PART, :] = grad_pre
        to[PART:, :] = grad_w[at(me["x"] ^ k, SLICE), :].astype(BF)


def output_body(aggregate, weight, output):
    preact = dot(aggregate[at(place()["h"], SLICE), :], weight[...])
    output[...] = (preact * jax.nn.sigmoid(preact)).astype(BF)


def backward_body(dense_t, weight, m0, m2, m3, m1, share, to_c, grad_agg, grad_pre):
    me = place()
    for k, m in enumerate((m0, m1, m2, m3)):
        grad_pre[at(me["x"] ^ k, PART), :] = m[0:PART, :]
    grad = dot(grad_pre[...], weight[...], ((1,), (1,))).astype(BF)
    grad_agg[...] = grad
    to_c[0:BLOCK, :] = dot(dense_t[3], grad)
    total = share[...] + m1[PART:, :].astype(F32)
    to_c[BLOCK:, :] = total + (m2[PART:, :].astype(F32) + m3[PART:, :].astype(F32))


def keep_body(dense_t, grad_agg, keep):
    keep[...] = dot(dense_t[2], grad_agg[...])


def to_u_body(keep, mine, got, u3, u2, u1, u0, share):
    me = place()
    for k, out in ((3, u3), (2, u2), (1, u1), (0, u0)):
        rows = at(me["z"] ^ k, PART)
        out[0:PART, :] = (keep[rows, :] + got[rows, :]).astype(BF)
    both = (mine[BLOCK:, :] + got[BLOCK:, :]).astype(BF)
    u3[PART:, :] = both
    share[...] = both


def kept_body(dense_t, grad_agg, to_c, keep):
    to_c[...] = dot(dense_t[1], grad_agg[...])
    keep[...] = dot(dense_t[0], grad_agg[...])


def after_c_body(keep, got, own, total):
    me = place()
    total[...] = keep[...] + got[...]
    for k in range(4):
        own[k * PART : (k + 1) * PART, :] = total[at(me["z"] ^ k, PART), :]


def to_z_body(k, own, got, share, earlier, to, pair):
    me = place()
    to[0:PART, :] = (own[k * PART : (k + 1) * PART, :] + got[0:PART, :].astype(F32)).astype(BF)
    pair[...] = share[...].astype(F32) + earlier[PART:, :].astype(F32)
    to[PART:, :] = pair[at(me["z"] ^ k, PIECE), :].astype(BF)


def to_z3_body(own, share, earlier, to, pair):
    to_z_body(3, own, earlier, share, earlier, to, pair)


def to_z2_body(own, got, share, earlier, to, pair):
    to_z_body(2, own, got, share, earlier, to, pair)


def to_z1_body(own, got, got_own, share, earlier, to, kept, pair):
    to_z_body(1, own, got, share, earlier, to, pair)
    kept[0:PART, :] = own[0:PART, :] + got_own[...].astype(F32)
    kept[PART:, :] = pair[at(place()["z"], PIECE), :]


def after_z_body(kept, r1, r2, r3, to_v):
    total = kept[...] + r1[...].astype(F32) + (r2[...].astype(F32) + r3[...].astype(F32))
    to_v[0:PART, :] = total[:PART].astype(BF)
    high, low = split(total[PART:])
    to_v[PART : PART + PIECE, :] = high
    to_v[PART + PIECE :, :] = low


def after_v_body(one, two, piece, share):
    piece[...] = (one[0:PART, :].astype(F32) + two[0:PART, :].astype(F32)).astype(BF)
    parts = [ref[PART : PART + PIECE, :].astype(F32) + ref[PART + PIECE :, :].astype(F32) for ref in (one, two)]
    high, low = split(parts[0] + parts[1])
    share[0:PIECE, :] = high
    share[PIECE:, :] = low


def last_body(piece, s0, s3, s2, s1, message):
    me = place()
    message[0:PART, :] = piece[...]
    for k, share in enumerate((s0, s1, s2, s3)):
        for half in range(2):
            start = pl.multiple_of(PART + half * SLICE + (me["z"] ^ k) * PIECE, PIECE)
            message[pl.ds(start, PIECE), :] = share[half * PIECE : (half + 1) * PIECE, :]


def finish_body(m0, m2, m3, m1, grad_features, grad_weight):
    me = place()
    for k, message in enumerate((m0, m1, m2, m3)):
        grad_features[at(chunk_of(me, me["x"] ^ k), PART), :] = message[0:PART, :]
        grad_weight[at(me["x"] ^ k, SLICE), :] = get_split(message, PART)


def on_device(features, weight, cotangent, tile_values, tile_slots, tile_count):
    part = ((PART, WIDTH), BF)
    part32 = ((PART, WIDTH), F32)
    block = ((BLOCK, WIDTH), BF)
    block32 = ((BLOCK, WIDTH), F32)
    share32 = ((SLICE, WIDTH), F32)
    share16 = ((SLICE, WIDTH), BF)
    two = ((2 * PART, WIDTH), BF)
    to_z = ((PART + SLICE, WIDTH), BF)
    dense_shape = ((4, BLOCK, BLOCK), BF)

    (half,) = call(half_body, [two], features, specs=[HBM], scratch=[pltpu.SemaphoreType.DMA])
    half = send(half, TO_COLUMN)
    dense, dense_t = call(
        dense_body, [dense_shape, dense_shape], tile_slots, tile_count, tile_values, specs=[SMEM, SMEM, VMEM]
    )
    half, dense, dense_t = lax.optimization_barrier((half, dense, dense_t))
    mine = [half, send(half, FLIP_Z[0])]
    by_u = [send(value, FLIP_U) for value in mine]
    by_c = [send(value, FLIP_C) for value in mine]
    by_uc = [send(value, FLIP_C) for value in by_u]
    total = pltpu.VMEM((BLOCK, WIDTH), F32)
    (most,) = call(
        forward_body, [block32], dense, *mine[::-1], *by_c[::-1], *by_u[::-1], scratch=[pltpu.VMEM((3, BLOCK, WIDTH), BF)]
    )
    *to, own = call(
        forward_last_body, [part, part, part, part32], dense, *by_uc[::-1], most, scratch=[pltpu.VMEM((1, BLOCK, WIDTH), BF), total]
    )
    got = [send(value, route) for value, route in zip(to, FAR_X)]
    (mine,) = call(sum_body, [to_z], own, got[1], got[2], got[0], cotangent)
    got = send(mine, FLIP_H)
    *to, own, aggregate, share = call(
        layer_body, [to_z, to_z, to_z, part, part, share32], mine, got, weight, scratch=[pltpu.VMEM((WIDTH, WIDTH), F32)]
    )
    (output,) = call(output_body, [((SLICE, WIDTH), BF)], aggregate, weight)
    got = [send(value, route) for value, route in zip(to, FAR_X)]
    to_c, grad_agg = call(
        backward_body, [((BLOCK + SLICE, WIDTH), F32), block], dense_t, weight, own, *got, share,
        scratch=[pltpu.VMEM((BLOCK, WIDTH), BF)],
    )
    got = send(to_c, FLIP_C)
    (keep_u,) = call(keep_body, [block32], dense_t, grad_agg)
    *to_u, share = call(to_u_body, [to_z, part, part, part, share16], keep_u, to_c, got)
    u3, u2, u1, u0 = [send(value, FLIP_U) for value in to_u]
    to_c, keep = call(kept_body, [block32, block32], dense_t, grad_agg)
    (own,) = call(after_c_body, [block32], keep, send(to_c, FLIP_C), scratch=[total])
    pair = [pltpu.VMEM((SLICE, WIDTH), F32)]
    to_z = ((PART + PIECE, WIDTH), BF)
    both32 = ((PART + PIECE, WIDTH), F32)
    (to3,) = call(to_z3_body, [to_z], own, share, u3, scratch=pair)
    (to2,) = call(to_z2_body, [to_z], own, u2, share, u3, scratch=pair)
    to1, kept = call(to_z1_body, [to_z, both32], own, u1, u0, share, u3, scratch=pair)
    from_z = [send(value, route) for value, route in zip((to1, to2, to3), FLIP_Z)]
    (to_v,) = call(after_z_body, [((PART + 2 * PIECE, WIDTH), BF)], kept, *from_z)
    piece, share = call(after_v_body, [part, ((2 * PIECE, WIDTH), BF)], to_v, send(to_v, FLIP_V))
    shares = [share] + [send(share, route) for route in FLIP_Z[::-1]]
    (message,) = call(last_body, [two], send(piece, TO_ROW), *shares)
    grad_features, grad_weight = call(finish_body, [block, ((WIDTH, WIDTH), F32)], message, *[send(message, route) for route in FAR_X])
    return output, grad_weight, grad_features


def solution(mesh):
    placed = (
        P("rows", None),
        P(),
        P(("rows", "rep"), None),
        P("rows", "rep", None, None, None),
        P("rows", "rep", None),
        P("rows", "rep"),
    )
    return jax.shard_map(
        on_device,
        mesh=mesh,
        in_specs=placed,
        out_specs=(P(("rows", "rep"), None), P(), P("rows", None)),
        check_vma=False,
    )
```

```python
import itertools

import jax
import jax.numpy as jnp
from jax import lax
from jax.experimental import pallas as pl
from jax.experimental.pallas import tpu as pltpu
from jax.sharding import PartitionSpec as P

BF = jnp.bfloat16
F32 = jnp.float32
TILE = 128
WIDTH = 256
BLOCK = 512
PART = 128
SLICE = 64
PIECE = 16
AXES = ("rows", "rep")


def u_of(y):
    return (y ^ (y >> 1)) & 1


def v_of(y):
    return y >> 1


Y_OF = {(u_of(y), v_of(y)): y for y in range(4)}
PLACES = list(itertools.product(range(4), range(4), range(2), range(4), range(2)))


def index_of(z, y, c, x, h):
    return (z * 8 + y * 2 + c) * 8 + x * 2 + h


def pairs(target):
    return [(index_of(*place), index_of(*target(*place))) for place in PLACES]


FLIP_C = pairs(lambda z, y, c, x, h: (z, y, 1 - c, x, h))
FLIP_U = pairs(lambda z, y, c, x, h: (z, Y_OF[1 - u_of(y), v_of(y)], c, x, h))
FLIP_V = pairs(lambda z, y, c, x, h: (z, Y_OF[u_of(y), 1 - v_of(y)], c, x, h))
FLIP_H = pairs(lambda z, y, c, x, h: (z, y, c, x, 1 - h))
FLIP_X = [pairs(lambda z, y, c, x, h, k=k: (z, y, c, x ^ k, h)) for k in (1, 2, 3)]
FLIP_Z = [pairs(lambda z, y, c, x, h, k=k: (z ^ k, y, c, x, h)) for k in (1, 2, 3)]
FAR_X = (FLIP_X[1], FLIP_X[2], FLIP_X[0])
ROUTE = (((2, 1, 3, 0), (0, 3, 2, 1), (2, 1, 0, 3), (3, 0, 2, 1)), ((0, 1, 3, 2), (0, 1, 2, 3), (0, 1, 2, 3), (1, 0, 2, 3)))
TO_ROW = pairs(lambda z, y, c, x, h: (x, Y_OF[u_of(y), h], c, ROUTE[v_of(y) == h][x][z], 1 - v_of(y)))
SERVED = (
    (2, 4, 0, 6, 5, 3, 1, 7), (2, 4, 0, 6, 5, 3, 1, 7), (6, 0, 4, 2, 5, 3, 1, 7), (6, 0, 4, 2, 5, 3, 1, 7),
    (5, 3, 7, 1, 2, 4, 6, 0), (5, 3, 7, 1, 2, 4, 6, 0), (1, 7, 5, 3, 2, 4, 6, 0), (1, 7, 5, 3, 2, 4, 6, 0),
    (5, 3, 4, 2, 0, 6, 7, 1), (5, 3, 4, 2, 0, 6, 7, 1), (5, 3, 0, 6, 2, 4, 7, 1), (5, 3, 0, 6, 2, 4, 7, 1),
    (2, 4, 3, 5, 7, 1, 0, 6), (2, 4, 3, 5, 7, 1, 0, 6), (2, 4, 3, 5, 7, 1, 0, 6), (2, 4, 3, 5, 7, 1, 0, 6),
    (1, 7, 6, 0, 2, 4, 3, 5), (1, 7, 6, 0, 2, 4, 3, 5), (1, 7, 6, 4, 2, 0, 3, 5), (1, 7, 6, 4, 2, 0, 3, 5),
    (6, 0, 1, 7, 5, 3, 4, 2), (6, 0, 1, 7, 5, 3, 4, 2), (6, 0, 7, 1, 5, 3, 4, 2), (6, 0, 7, 1, 5, 3, 4, 2),
    (7, 1, 3, 5, 6, 0, 4, 2), (7, 1, 3, 5, 6, 0, 4, 2), (5, 3, 7, 1, 0, 6, 4, 2), (5, 3, 7, 1, 0, 6, 4, 2),
    (0, 6, 4, 2, 1, 7, 3, 5), (0, 6, 4, 2, 1, 7, 3, 5), (2, 4, 0, 6, 1, 7, 3, 5), (2, 4, 0, 6, 1, 7, 3, 5),
)


def served(z, y, c, x, h):
    replica = SERVED[x * 8 + h * 4 + u_of(y) * 2 + c][z * 2 + v_of(y)]
    return x, Y_OF[u_of(y), h], c, replica >> 1, replica & 1


TO_COLUMN = [(there, here) for here, there in pairs(served)]


def half_words():
    words = [0] * 8
    for there, here in TO_COLUMN:
        words[there >> 5] |= (here >> 6 & 1) << (there & 31)
    return [word - (1 << 32) if word >> 31 else word for word in words]


HALVES = half_words()


def chunk_table(same):
    word = sum((z << (8 * x + 2 * ROUTE[same][x][z])) for x in range(4) for z in range(4))
    return word - (1 << 32) if word >> 31 else word


CHUNKS = (chunk_table(0), chunk_table(1))


def send(value, route):
    return lax.ppermute(value, AXES, route)


def place():
    r = lax.axis_index("rows")
    p = lax.axis_index("rep")
    y = (r >> 1) & 3
    v = y >> 1
    return dict(z=r >> 3, c=r & 1, u=(y ^ v) & 1, v=v, x=p >> 1, h=p & 1)


def chunk_of(me, x):
    word = jnp.where((1 - me["h"]) == me["v"], jnp.int32(CHUNKS[1]), jnp.int32(CHUNKS[0]))
    return (word >> (8 * me["z"] + 2 * x)) & 3


def at(index, size):
    return pl.ds(pl.multiple_of(index * size, size), size)


def dot(a, b, dims=((1,), (0,))):
    return lax.dot_general(a, b, (dims, ((), ())), preferred_element_type=F32)


SMEM = pl.BlockSpec(memory_space=pltpu.SMEM)
VMEM = pl.BlockSpec(memory_space=pltpu.VMEM)
HBM = pl.BlockSpec(memory_space=pl.ANY)


def call(body, outs, *args, specs=None, scratch=()):
    return pl.pallas_call(
        body,
        out_shape=[jax.ShapeDtypeStruct(shape, dtype) for shape, dtype in outs],
        in_specs=specs or [VMEM] * len(args),
        out_specs=[VMEM] * len(outs),
        scratch_shapes=list(scratch),
        compiler_params=pltpu.CompilerParams(vmem_limit_bytes=24 * 2**20),
    )(*args)


def split(value):
    high = value.astype(BF)
    return high, (value - high.astype(F32)).astype(BF)


def put_split(ref, start, value):
    high, low = split(value)
    ref[start : start + SLICE, :] = high
    ref[start + SLICE : start + 2 * SLICE, :] = low


def get_split(ref, start):
    return ref[start : start + SLICE, :].astype(F32) + ref[start + SLICE : start + 2 * SLICE, :].astype(F32)


def half_body(features, out, sem):
    device = lax.axis_index("rows") * 8 + lax.axis_index("rep")
    word = jnp.int32(0)
    for i, value in enumerate(HALVES):
        word = jnp.where(device >> 5 == i, jnp.int32(value), word)
    half = (word >> (device & 31)) & 1
    copy = pltpu.make_async_copy(features.at[at(half, 2 * PART), :], out, sem)
    copy.start()
    copy.wait()


def dense_body(slots, count, tiles, dense, dense_t):
    me = place()
    dense[...] = jnp.zeros_like(dense)
    dense_t[...] = jnp.zeros_like(dense_t)
    for k in range(4):
        b = ((me["u"] ^ me["h"]) * 2 + me["c"]) ^ k
        for s in range(2):
            slot = slots[0, b, s]
            tile = jnp.where(s < count[0, b], tiles[0, b, s], jnp.zeros((), BF))

            @pl.when(s < count[0, b])
            def _():
                dense[k, at(slot >> 2, TILE), at(slot & 3, TILE)] = tile
                dense_t[k, at(slot & 3, TILE), at(slot >> 2, TILE)] = tile.T


def put_block(me, blocks, i, mine, other):
    half = me["z"] & 1
    blocks[i, at(half, 2 * PART), :] = mine[...]
    blocks[i, at(1 - half, 2 * PART), :] = other[...]


def forward_body(dense, b0, a0, b1, a1, b2, a2, total, blocks):
    me = place()
    for i, (first, second) in enumerate(((a0, b0), (a1, b1), (a2, b2))):
        put_block(me, blocks, i, first, second)
    total[...] = dot(dense[0], blocks[0]) + dot(dense[1], blocks[1]) + dot(dense[2], blocks[2])


def forward_last_body(dense, b3, a3, most, to2, to3, to1, own, blocks, total):
    me = place()
    put_block(me, blocks, 0, a3, b3)
    total[...] = most[...] + dot(dense[3], blocks[0])
    for k, to in enumerate((own, to1, to2, to3)):
        to[...] = total[at(me["x"] ^ k, PART), :].astype(to.dtype)


def sum_body(own, r3, r1, r2, cot, to_h):
    total = own[...] + r1[...].astype(F32) + (r2[...].astype(F32) + r3[...].astype(F32))
    to_h[0:PART, :] = total.astype(BF)
    to_h[PART:, :] = cot[...]


def aggregate_of(mine, got):
    return (mine[0:PART, :].astype(F32) + got[0:PART, :].astype(F32)).astype(BF)


def layer_body(mine, got, weight, to2, to3, to1, own, aggregate, share, grad_w):
    me = place()
    agg = aggregate_of(mine, got)
    preact = dot(agg, weight[...])
    gates = jax.nn.sigmoid(preact)
    first = me["h"] == 0
    a, b = mine[PART:, :], got[PART:, :]
    cotangent = jnp.concatenate([jnp.where(first, a, b), jnp.where(first, b, a)], axis=0).astype(F32)
    grad_pre = (cotangent * gates * (1.0 + preact * (1.0 - gates))).astype(BF)
    grad_w[...] = dot(agg, grad_pre, ((0,), (0,)))
    aggregate[...] = agg
    own[...] = grad_pre
    share[...] = grad_w[at(me["x"], SLICE), :]
    for k, to in ((3, to3), (2, to2), (1, to1)):
        to[0:PART, :] = grad_pre
        to[PART:, :] = grad_w[at(me["x"] ^ k, SLICE), :].astype(BF)


def output_body(aggregate, weight, output):
    preact = dot(aggregate[at(place()["h"], SLICE), :], weight[...])
    output[...] = (preact * jax.nn.sigmoid(preact)).astype(BF)


def backward_body(dense_t, weight, m0, m2, m3, m1, share, to_c, grad_agg, grad_pre):
    me = place()
    for k, m in enumerate((m0, m1, m2, m3)):
        grad_pre[at(me["x"] ^ k, PART), :] = m[0:PART, :]
    grad = dot(grad_pre[...], weight[...], ((1,), (1,))).astype(BF)
    grad_agg[...] = grad
    to_c[0:BLOCK, :] = dot(dense_t[3], grad).astype(BF)
    total = share[...] + m1[PART:, :].astype(F32)
    put_split(to_c, BLOCK, total + (m2[PART:, :].astype(F32) + m3[PART:, :].astype(F32)))


def keep_body(dense_t, grad_agg, keep):
    keep[...] = dot(dense_t[2], grad_agg[...])


def to_u_body(keep, mine, got, u3, u2, u1, u0, share):
    me = place()
    for k, out in ((3, u3), (2, u2), (1, u1), (0, u0)):
        rows = at(me["z"] ^ k, PART)
        out[0:PART, :] = (keep[rows, :] + got[rows, :].astype(F32)).astype(BF)
    both = (get_split(mine, BLOCK) + get_split(got, BLOCK)).astype(BF)
    u3[PART:, :] = both
    share[...] = both


def kept_body(dense_t, grad_agg, to_c, keep):
    to_c[...] = dot(dense_t[1], grad_agg[...]).astype(BF)
    keep[...] = dot(dense_t[0], grad_agg[...])


def after_c_body(keep, got, own, total):
    me = place()
    total[...] = keep[...] + got[...].astype(F32)
    for k in range(4):
        own[k * PART : (k + 1) * PART, :] = total[at(me["z"] ^ k, PART), :]


def to_z_body(k, own, got, share, earlier, to, pair):
    me = place()
    to[0:PART, :] = (own[k * PART : (k + 1) * PART, :] + got[0:PART, :].astype(F32)).astype(BF)
    pair[...] = share[...].astype(F32) + earlier[PART:, :].astype(F32)
    to[PART:, :] = pair[at(me["z"] ^ k, PIECE), :].astype(BF)


def to_z3_body(own, share, earlier, to, pair):
    to_z_body(3, own, earlier, share, earlier, to, pair)


def to_z2_body(own, got, share, earlier, to, pair):
    to_z_body(2, own, got, share, earlier, to, pair)


def to_z1_body(own, got, got_own, share, earlier, to, kept, pair):
    to_z_body(1, own, got, share, earlier, to, pair)
    kept[0:PART, :] = own[0:PART, :] + got_own[...].astype(F32)
    kept[PART:, :] = pair[at(place()["z"], PIECE), :]


def after_z_body(kept, r1, r2, r3, to_v):
    total = kept[...] + r1[...].astype(F32) + (r2[...].astype(F32) + r3[...].astype(F32))
    to_v[0:PART, :] = total[:PART].astype(BF)
    high, low = split(total[PART:])
    to_v[PART : PART + PIECE, :] = high
    to_v[PART + PIECE :, :] = low


def after_v_body(one, two, piece, share):
    piece[...] = (one[0:PART, :].astype(F32) + two[0:PART, :].astype(F32)).astype(BF)
    parts = [ref[PART : PART + PIECE, :].astype(F32) + ref[PART + PIECE :, :].astype(F32) for ref in (one, two)]
    high, low = split(parts[0] + parts[1])
    share[0:PIECE, :] = high
    share[PIECE:, :] = low


def last_body(piece, s0, s3, s2, s1, message):
    me = place()
    message[0:PART, :] = piece[...]
    for k, share in enumerate((s0, s1, s2, s3)):
        for half in range(2):
            start = pl.multiple_of(PART + half * SLICE + (me["z"] ^ k) * PIECE, PIECE)
            message[pl.ds(start, PIECE), :] = share[half * PIECE : (half + 1) * PIECE, :]


def finish_body(m0, m2, m3, m1, grad_features, grad_weight):
    me = place()
    for k, message in enumerate((m0, m1, m2, m3)):
        grad_features[at(chunk_of(me, me["x"] ^ k), PART), :] = message[0:PART, :]
        grad_weight[at(me["x"] ^ k, SLICE), :] = get_split(message, PART)


def on_device(features, weight, cotangent, tile_values, tile_slots, tile_count):
    part = ((PART, WIDTH), BF)
    part32 = ((PART, WIDTH), F32)
    block = ((BLOCK, WIDTH), BF)
    block32 = ((BLOCK, WIDTH), F32)
    share32 = ((SLICE, WIDTH), F32)
    share16 = ((SLICE, WIDTH), BF)
    two = ((2 * PART, WIDTH), BF)
    to_z = ((PART + SLICE, WIDTH), BF)
    dense_shape = ((4, BLOCK, BLOCK), BF)

    (half,) = call(half_body, [two], features, specs=[HBM], scratch=[pltpu.SemaphoreType.DMA])
    half = send(half, TO_COLUMN)
    dense, dense_t = call(
        dense_body, [dense_shape, dense_shape], tile_slots, tile_count, tile_values, specs=[SMEM, SMEM, VMEM]
    )
    half, dense, dense_t = lax.optimization_barrier((half, dense, dense_t))
    mine = [half, send(half, FLIP_Z[0])]
    by_u = [send(value, FLIP_U) for value in mine]
    by_c = [send(value, FLIP_C) for value in mine]
    by_uc = [send(value, FLIP_C) for value in by_u]
    total = pltpu.VMEM((BLOCK, WIDTH), F32)
    (most,) = call(
        forward_body, [block32], dense, *mine[::-1], *by_c[::-1], *by_u[::-1], scratch=[pltpu.VMEM((3, BLOCK, WIDTH), BF)]
    )
    *to, own = call(
        forward_last_body, [part, part, part, part32], dense, *by_uc[::-1], most, scratch=[pltpu.VMEM((1, BLOCK, WIDTH), BF), total]
    )
    got = [send(value, route) for value, route in zip(to, FAR_X)]
    (mine,) = call(sum_body, [to_z], own, got[1], got[2], got[0], cotangent)
    got = send(mine, FLIP_H)
    *to, own, aggregate, share = call(
        layer_body, [to_z, to_z, to_z, part, part, share32], mine, got, weight, scratch=[pltpu.VMEM((WIDTH, WIDTH), F32)]
    )
    (output,) = call(output_body, [((SLICE, WIDTH), BF)], aggregate, weight)
    got = [send(value, route) for value, route in zip(to, FAR_X)]
    to_c, grad_agg = call(
        backward_body, [((BLOCK + 2 * SLICE, WIDTH), BF), block], dense_t, weight, own, *got, share,
        scratch=[pltpu.VMEM((BLOCK, WIDTH), BF)],
    )
    got = send(to_c, FLIP_C)
    (keep_u,) = call(keep_body, [block32], dense_t, grad_agg)
    *to_u, share = call(to_u_body, [to_z, part, part, part, share16], keep_u, to_c, got)
    u3, u2, u1, u0 = [send(value, FLIP_U) for value in to_u]
    to_c, keep = call(kept_body, [block, block32], dense_t, grad_agg)
    (own,) = call(after_c_body, [block32], keep, send(to_c, FLIP_C), scratch=[total])
    pair = [pltpu.VMEM((SLICE, WIDTH), F32)]
    to_z = ((PART + PIECE, WIDTH), BF)
    both32 = ((PART + PIECE, WIDTH), F32)
    (to3,) = call(to_z3_body, [to_z], own, share, u3, scratch=pair)
    (to2,) = call(to_z2_body, [to_z], own, u2, share, u3, scratch=pair)
    to1, kept = call(to_z1_body, [to_z, both32], own, u1, u0, share, u3, scratch=pair)
    from_z = [send(value, route) for value, route in zip((to1, to2, to3), FLIP_Z)]
    (to_v,) = call(after_z_body, [((PART + 2 * PIECE, WIDTH), BF)], kept, *from_z)
    piece, share = call(after_v_body, [part, ((2 * PIECE, WIDTH), BF)], to_v, send(to_v, FLIP_V))
    shares = [share] + [send(share, route) for route in FLIP_Z[::-1]]
    (message,) = call(last_body, [two], send(piece, TO_ROW), *shares)
    grad_features, grad_weight = call(finish_body, [block, ((WIDTH, WIDTH), F32)], message, *[send(message, route) for route in FAR_X])
    return output, grad_weight, grad_features


def solution(mesh):
    placed = (
        P("rows", None),
        P(),
        P(("rows", "rep"), None),
        P("rows", "rep", None, None, None),
        P("rows", "rep", None),
        P("rows", "rep"),
    )
    return jax.shard_map(
        on_device,
        mesh=mesh,
        in_specs=placed,
        out_specs=(P(("rows", "rep"), None), P(), P("rows", None)),
        check_vma=False,
    )
```
